1024 devices in a mesh: expert: 64 (over z, core), fsdp: 16 (over x, y).
Axes of the slice: x: 4, y: 4, z: 32, core: 2. Of those that a mesh axis runs over, the one named last changes fastest.
Arguments:
- tokens: bfloat16 [2048, 2048], P('expert', 'fsdp'), may hold values from -6 to 6
- target: bfloat16 [2048, 2048], P('expert', 'fsdp'), may hold values from -6 to 6
- expert_ids: int32 [2048, 8], P('expert'), may hold values from 0 to 63, all different within a row; in each aligned block of 32 rows (0 to 31, 32 to 63, ...) at most 7 rows name the same one
- route_weights: float32 [2048, 8], P('expert'), may hold values from 0.05 to 0.3
- w_gate: bfloat16 [64, 768, 2048], P('expert', 'fsdp'), may hold values from -0.1875 to 0.1875
- w_up: bfloat16 [64, 768, 2048], P('expert', 'fsdp'), may hold values from -0.1875 to 0.1875
- w_down: bfloat16 [64, 768, 2048], P('expert', 'fsdp'), may hold values from -0.3125 to 0.3125
Outputs:
- layer_out: bfloat16 [2048, 2048], P('expert', 'fsdp')
- grad_tokens: bfloat16 [2048, 2048], P('expert', 'fsdp')
- grad_route: float32 [2048, 8], P('expert')
- grad_gate: float32 [64, 768, 2048], P('expert', 'fsdp')
- grad_up: float32 [64, 768, 2048], P('expert', 'fsdp')
- grad_down: float32 [64, 768, 2048], P('expert', 'fsdp')
The draws below stay inside these ranges and needn't reach their ends.
Inputs may be any that keep to these rules, and one draw needn't show every extreme that they name: `expert_ids`: each row names 8 different experts. In each aligned block of 32 rows (the rows of one index of the expert axis) no expert is named by more than 7 rows, a bound that some block reaches.
All inputs are finite; a program needn't handle non-finite values.
Results may differ from the reference program's by a relative error of at most 0.022.
Values may be sent and summed in bfloat16 or wider, within the bound.
No kernel may reach another device: no remote copies, remote signals or barrier semaphores. Data moves between devices by JAX's collectives and lax.ppermute only.
A program may use at most 64 MiB of HBM per device.

```python
import math
import jax
import jax.numpy as jnp
import numpy as np
from jax import lax

D = 2048
FF = 768
TOPK = 8
GROUP = 32
TOKENS = 2048
EXPERTS = 64
FS = 48
CAP = 7
N_FSDP = 16


def spiked(drawn, own_key, source, target, blocks, factor):
    def block_of(position):
        return (jnp.arange(drawn.shape[position]) // (drawn.shape[position] // blocks)).reshape((-1,) + (1,) * (drawn.ndim - 1 - position))

    near = jax.random.permutation(own_key, blocks)[block_of(target)]
    second = (block_of(target) + blocks // 2) % blocks
    return jnp.where((block_of(source) == near) | (block_of(source) == second), factor * drawn, drawn)


def block_scale(stream_key, shape, cuts, least, largest):
    loudness, own = 1.0, jax.random.fold_in(stream_key, 6)
    for position, blocks in cuts:
        heights = jnp.exp(jax.random.uniform(jax.random.fold_in(own, position), (blocks,), jnp.float32, least / len(cuts), largest / len(cuts)))
        loudness = loudness * jnp.repeat(heights, shape[position] // blocks).reshape([-1 if axis == position else 1 for axis in range(len(shape))])
    return loudness


def shared_out(stream_key, own, number, rows, amount, top, most, lean):
    sequence = jax.random.permutation(stream_key, amount)
    heavy_load, usual = load_shares(amount, rows * top, most, lean, True), load_shares(amount, rows * top, most, lean, False)
    places = jnp.arange(amount)

    def named(lengths, offset_by):
        used = int((lengths > 0).sum())
        fixed = max(1, used // 4)
        shifted = fixed + (places - fixed + offset_by * (used - fixed)) % max(1, amount - fixed)
        return jnp.zeros((amount,), jnp.int32).at[sequence[jnp.where(places < fixed, places, shifted)]].set(jnp.asarray(lengths, jnp.int32))

    lengths = jnp.where(number % 4 == 0, named(heavy_load, number // 4), named(usual, number - number // 4 - 1))
    mixed = jax.random.permutation(jax.random.fold_in(own, 3), amount)
    source_of, taker = mixed[0:amount // 2 * 2:2], mixed[1:amount // 2 * 2:2]
    room = jnp.minimum(lengths[source_of] - 1, most - lengths[taker]) // 2
    room = jnp.where((source_of == sequence[0]) | (taker == sequence[0]) | (lengths[taker] == 0), 0, jnp.maximum(room, 0))
    shifted = jax.random.randint(jax.random.fold_in(own, 4), (amount // 2,), 0, 1 << 20) % (room + 1)
    lengths = lengths.at[source_of].add(-shifted).at[taker].add(shifted)
    labels = jnp.searchsorted(jnp.cumsum(lengths), jnp.arange(rows * top), side="right").astype(jnp.int32)
    table = labels.reshape(top, rows).T
    table = table[jax.random.permutation(jax.random.fold_in(own, 1), rows)]
    offset_by = jax.random.randint(jax.random.fold_in(own, 2), (rows, 1), 0, top)
    return jnp.take_along_axis(table, (jnp.arange(top)[None, :] + offset_by) % top, axis=1)


def load_shares(amount, total, bound, lean, full):
    loads = [(1 << 20) // math.isqrt(rank ** lean) + 1 for rank in range(1, amount + 1)]
    largest = bound if full else min(bound, max(-(-total // amount), total * loads[0] // sum(loads)))
    least = 1 if total - largest >= amount - 1 else 0
    holding, rest = [largest] + [least] * (amount - 1), total - largest - least * (amount - 1)
    while rest > 0:
        free = [i for i in range(1, amount) if holding[i] < largest] or [i for i in range(1, amount) if holding[i] < bound]
        whole, remaining = sum([loads[i] for i in free]), rest
        for i in free:
            more = min(bound - holding[i], max(1, remaining * loads[i] // whole), rest)
            holding[i] = holding[i] + more
            rest = rest - more
    return np.array(holding)


def normal_values(own_key, extent, scale, reach, shards=(), held_as=jnp.bfloat16):
    gain = block_scale(own_key, extent, shards, -0.22, 0.18) if shards else 1.0
    array = jax.random.normal(own_key, extent, jnp.float32) * scale * gain
    return jnp.minimum(jnp.maximum(array, -reach), reach).astype(held_as)


def bell_draw_with(rng, shape, deviation, reach, cuts, heavy, kind=jnp.bfloat16):
    array = deviation * jax.random.normal(rng, shape, jnp.float32)
    if cuts:
        array = array * block_scale(rng, shape, cuts, -0.22, 0.18)
    return jnp.clip(spiked(array, jax.random.fold_in(rng, 3), *heavy), -reach, reach).astype(kind)


def setup_inputs(seed: int = 0) -> dict:
    key_list = jax.random.split(jax.random.key(seed), 8)
    tokens = normal_values(key_list[0], (TOKENS, D), 1.0, 6.0, ((0, 64), (1, 16)))
    target = normal_values(key_list[1], (TOKENS, D), 1.0, 6.0, ((0, 64), (1, 16)))
    expert_ids_keys = jax.random.split(jax.random.fold_in(key_list[2], 1), TOKENS // GROUP)
    expert_ids_turns = jax.random.permutation(jax.random.fold_in(key_list[2], 3), TOKENS // GROUP)
    expert_ids = jax.vmap(lambda own, number: shared_out(jax.random.fold_in(key_list[2], 2), own, number, GROUP, EXPERTS, TOPK, CAP, 2))(expert_ids_keys, expert_ids_turns).reshape((TOKENS, TOPK))
    route_weights = jnp.clip(0.05 + 0.25 * jax.random.uniform(key_list[3], (TOKENS, TOPK), jnp.float32) ** block_scale(key_list[3], (TOKENS, TOPK), ((0, 64),), -0.2, 0.2), 0.05, 0.3)
    w_gate = bell_draw_with(key_list[4], (EXPERTS, FF, D), D ** -0.5, 0.1875, ((0, 64), (1, 16)), (1, 2, 16, 2.0))
    w_up = bell_draw_with(key_list[5], (EXPERTS, FF, D), D ** -0.5, 0.1875, ((0, 64), (1, 16)), (1, 2, 16, 2.0))
    w_down = bell_draw_with(key_list[6], (EXPERTS, FF, D), FF ** -0.5, 0.3125, ((0, 64), (1, 16)), (1, 2, 16, 2.0))
    return {"tokens": tokens, "target": target, "expert_ids": expert_ids, "route_weights": route_weights, "w_gate": w_gate, "w_up": w_up, "w_down": w_down}


def route_rows(expert_ids):
    blocks = TOKENS // GROUP
    flat_ids = expert_ids.reshape(blocks, GROUP * TOPK)
    onehot = (flat_ids[:, :, None] == jnp.arange(EXPERTS, dtype=jnp.int32)[None, None, :]).astype(jnp.int32)
    before = jnp.cumsum(onehot, axis=1) - onehot
    route_rank = jnp.sum(before * onehot, axis=2)
    base = jnp.arange(blocks, dtype=jnp.int32)[:, None] * CAP
    return (base + route_rank).reshape(TOKENS, TOPK).astype(jnp.int32)


def sliced_product(left, weight):
    pieces = left.astype(jnp.float32).reshape(left.shape[0], N_FSDP, FS)
    blocks = weight.astype(jnp.float32).reshape(N_FSDP, FS, D)
    return jnp.einsum("rjh,jhd->rjd", pieces, blocks)


def rounded_sum(parts):
    kept = lax.optimization_barrier(parts.astype(jnp.bfloat16))
    return jnp.sum(kept.astype(jnp.float32), axis=1)


def expert_pass(rows, gate_w, up_w):
    gate_pre = jnp.dot(rows, gate_w.T, preferred_element_type=jnp.float32)
    up_pre = jnp.dot(rows, up_w.T, preferred_element_type=jnp.float32)
    sigmoid_gate = jax.nn.sigmoid(gate_pre)
    hidden = (gate_pre * sigmoid_gate * up_pre).astype(jnp.bfloat16)
    return gate_pre, up_pre, sigmoid_gate, hidden


def reference(tokens, target, expert_ids, route_weights, w_gate, w_up, w_down):
    row_of = route_rows(expert_ids)
    width = (TOKENS // GROUP) * CAP
    spread = jnp.broadcast_to(tokens[:, None, :], (TOKENS, TOPK, D))
    grid_rows = jnp.zeros((EXPERTS, width, D), jnp.bfloat16).at[expert_ids, row_of].set(spread)

    def forward_one(operands):
        rows, gate_w, up_w, down_w = operands
        gate_pre, up_pre, sigmoid_gate, hidden = expert_pass(rows, gate_w, up_w)
        return rounded_sum(sliced_product(hidden, down_w))

    grid_out = lax.map(forward_one, (grid_rows, w_gate, w_up, w_down))
    route_out = grid_out[expert_ids, row_of]
    layer_out = jnp.sum(route_weights[:, :, None] * route_out, axis=1).astype(jnp.bfloat16)
    resid = (layer_out.astype(jnp.float32) - target.astype(jnp.float32)).astype(jnp.bfloat16)
    resid_wide = resid.astype(jnp.float32)
    grad_route = jnp.sum(resid_wide[:, None, :] * route_out, axis=2)
    scaled = (route_weights[:, :, None] * resid_wide[:, None, :]).astype(jnp.bfloat16)
    grid_scaled = jnp.zeros((EXPERTS, width, D), jnp.bfloat16).at[expert_ids, row_of].set(scaled)

    def backward_one(operands):
        rows, scaled_rows, gate_w, up_w, down_w = operands
        gate_pre, up_pre, sigmoid_gate, hidden = expert_pass(rows, gate_w, up_w)
        delta_hidden = jnp.dot(scaled_rows, down_w.T, preferred_element_type=jnp.float32)
        delta_gate = (delta_hidden * up_pre * sigmoid_gate * (1.0 + gate_pre * (1.0 - sigmoid_gate))).astype(jnp.bfloat16)
        delta_up = (delta_hidden * gate_pre * sigmoid_gate).astype(jnp.bfloat16)
        gate_grad = jnp.dot(delta_gate.T, rows, preferred_element_type=jnp.float32)
        up_grad = jnp.dot(delta_up.T, rows, preferred_element_type=jnp.float32)
        down_grad = jnp.dot(hidden.T, scaled_rows, preferred_element_type=jnp.float32)
        back_rows = rounded_sum(sliced_product(delta_gate, gate_w) + sliced_product(delta_up, up_w))
        return gate_grad, up_grad, down_grad, back_rows

    grad_gate, grad_up, grad_down, grid_back = lax.map(backward_one, (grid_rows, grid_scaled, w_gate, w_up, w_down))
    grad_tokens = jnp.sum(grid_back[expert_ids, row_of], axis=1).astype(jnp.bfloat16)
    return (layer_out, grad_tokens, grad_route, grad_gate, grad_up, grad_down)
```

```python
import functools

import jax
import jax.numpy as jnp
from jax import lax
from jax.experimental import pallas as pl
from jax.experimental.pallas import tpu as pltpu
from jax.sharding import Mesh, PartitionSpec as P

BF = jnp.bfloat16
F4 = jnp.float32
LANES = 128
HI = 8
CAP = 7


def dot(a, b, ca=1, cb=0):
    return lax.dot_general(a, b, (((ca,), (cb,)), ((), ())), preferred_element_type=F4)


def call(body, outs, *args, smem=(), flops=1e8, name=None):
    specs = [
        pl.BlockSpec(memory_space=pltpu.SMEM if i in smem else pltpu.VMEM)
        for i in range(len(args))
    ]
    nbytes = sum(a.size * a.dtype.itemsize for a in args)
    shapes = [jax.ShapeDtypeStruct(s, d) for s, d in outs]
    return pl.pallas_call(
        body,
        out_shape=shapes,
        in_specs=specs,
        out_specs=[pl.BlockSpec(memory_space=pltpu.VMEM) for _ in shapes],
        compiler_params=pltpu.CompilerParams(vmem_limit_bytes=40 * 1024 * 1024),
        cost_estimate=pl.CostEstimate(
            flops=int(flops), bytes_accessed=int(nbytes), transcendentals=0
        ),
        name=name,
    )(*args)


def lane(shape):
    return lax.broadcasted_iota(jnp.int32, shape, 1)


def roll(x, by):
    by = by % LANES
    return x if by == 0 else pltpu.roll(x, by, 1)


def split3(x, step):
    hi = x.astype(BF).astype(F4)
    rest = x - hi
    mid = rest.astype(BF).astype(F4)
    return hi + roll(mid, step) + roll(rest - mid, 2 * step)


def join3(x, step):
    return x + roll(x, -step) + roll(x, -2 * step)


def column_tile(column, h):
    at = lane((h, LANES))
    tile = jnp.zeros((h, LANES), F4)
    for c in range(CAP):
        tile = jnp.where(at == c, column[c * h : (c + 1) * h], tile)
    return tile


def scale_rows(rows, tile, h):
    return jnp.concatenate(
        [rows[c * h : (c + 1) * h] * tile[:, c : c + 1] for c in range(CAP)], axis=0
    )


def blocks_to_rows(x):
    return jnp.concatenate(
        [x[:, i * LANES : (i + 1) * LANES] for i in range(x.shape[1] // LANES)], axis=0
    )


def rows_to_blocks(x, rows):
    return jnp.concatenate(
        [x[i * rows : (i + 1) * rows] for i in range(x.shape[0] // rows)], axis=1
    )


def dispatch_body(base_ref, r_ref, m_ref, p_ref, ids_ref):
    h, l = r_ref.shape[0], m_ref.shape[0]
    g = 32
    width = h * g
    per = LANES // g
    at = lane((8, LANES))
    metas = [r_ref[i].astype(F4)[g : g + 8] for i in range(h)]

    def gathered(parts, start):
        out = []
        for q in range(h // per):
            acc = jnp.zeros((8, LANES), F4)
            for i in range(per):
                moved = roll(parts[q * per + i], i * g - start)
                acc = jnp.where(at // g == i, moved, acc)
            out.append(acc)
        return jnp.concatenate(out, axis=1)

    ids = gathered(metas, 0)
    weights = gathered([join3(m, g) for m in metas], g)
    ids_ref[...] = ids
    mine = (lax.broadcasted_iota(jnp.int32, (l, width), 0) + base_ref[0]).astype(F4)
    named = jnp.zeros((l, width), F4)
    weight_at = jnp.zeros((l, width), F4)
    for k in range(8):
        hit = ids[k : k + 1] == mine
        named = named + jnp.where(hit, 1.0, 0.0)
        weight_at = weight_at + jnp.where(hit, weights[k : k + 1], 0.0)
    row = lax.broadcasted_iota(jnp.int32, (width, width), 0)
    col = lane((width, width))
    before = jnp.where((row // g == col // g) & (row < col), 1.0, 0.0).astype(BF)
    rank = dot(named.astype(BF), before)
    rank = jnp.where(named > 0.0, rank, -1.0)
    block = lane((h, width)) // g == lax.broadcasted_iota(jnp.int32, (h, width), 0)
    x = jnp.concatenate([r_ref[i][:g] for i in range(h)], axis=0)
    for e in range(l):
        own = jnp.broadcast_to(rank[e : e + 1], (h, width))
        place = jnp.concatenate(
            [jnp.where(block & (own == float(c)), 1.0, 0.0) for c in range(8)], axis=0
        )
        column = jnp.sum(place * weight_at[e : e + 1], axis=1, keepdims=True)
        place = place.astype(BF)
        p_ref[e] = place
        rows = dot(place, x)
        tile = split3(column_tile(column, h), 8)
        m_ref[e] = jnp.concatenate([rows[: CAP * h], tile], axis=0).astype(BF)


def expert_in_body(r_ref, wg_ref, wu_ref, wd_ref, f_ref, w_ref):
    l, h = r_ref.shape[0], r_ref.shape[1] // 8
    fs = wg_ref.shape[0]
    rows = []
    for e in range(l):
        v = r_ref[e].astype(F4)
        rows.append(v[: CAP * h])
        w_ref[e] = join3(v[CAP * h :], 8)
    x = jnp.concatenate(rows, axis=0).astype(BF)
    for d in range(f_ref.shape[0]):
        part = pl.ds(d * LANES, LANES)
        f_ref[d, 0:fs] = wg_ref[:, part]
        f_ref[d, fs : 2 * fs] = wu_ref[:, part]
        f_ref[d, 2 * fs : 3 * fs] = wd_ref[:, part]
        f_ref[d, 3 * fs :] = x


def hidden_body(r_ref, wg_ref, wu_ref, gate_ref, up_ref, f_ref):
    n, fs = r_ref.shape[0], wg_ref.shape[0]
    slots = gate_ref.shape[1]
    held = r_ref.shape[1] - 3 * fs
    pad = jnp.zeros((slots - held, 2 * LANES), BF)
    total = jnp.zeros((2 * fs, slots), F4)
    for i in range(n // 2):
        x = jnp.concatenate([r_ref[2 * i, 3 * fs :], r_ref[2 * i + 1, 3 * fs :]], axis=1)
        x = jnp.concatenate([x, pad], axis=0)
        part = pl.ds(2 * i * LANES, 2 * LANES)
        w = jnp.concatenate([wg_ref[:, part], wu_ref[:, part]], axis=0)
        total = total + dot(w, x, 1, 1)
    gate, up = total[:fs], total[fs:]
    gate_ref[...] = gate
    up_ref[...] = up
    hidden = (gate * jax.nn.sigmoid(gate) * up).astype(BF)
    message = blocks_to_rows(hidden)
    for d in range(n):
        f_ref[d] = message


def expert_out_body(r_ref, wd_ref, w_ref, out_ref, h_ref, m_ref):
    n, fs = r_ref.shape[0], r_ref.shape[1] // 4
    l, h = w_ref.shape[0], w_ref.shape[1]
    hidden = jnp.concatenate([rows_to_blocks(r_ref[i], fs) for i in range(n)], axis=0)
    h_ref[...] = hidden
    out = dot(hidden, wd_ref[...], 0, 0)
    out_ref[...] = out
    for e in range(l):
        rows = out[e * CAP * h : (e + 1) * CAP * h]
        rows = scale_rows(rows, w_ref[e], h)
        m_ref[e] = jnp.concatenate([rows, jnp.zeros((h, LANES), F4)], axis=0).astype(BF)


def combine_body(r_ref, p_ref, m_ref):
    l, rows = r_ref.shape[0], r_ref.shape[1]
    x = jnp.concatenate([r_ref[i] for i in range(l)], axis=0)
    p = jnp.concatenate([p_ref[i] for i in range(l)], axis=0)
    y = dot(p, x, 0, 0).astype(BF)
    g = m_ref.shape[1]
    for i in range(m_ref.shape[0]):
        m_ref[i] = y[i * g : (i + 1) * g]


def resid_body(r_ref, t_ref, o_ref, m_ref):
    total = r_ref[0].astype(F4)
    for i in range(1, r_ref.shape[0]):
        total = total + r_ref[i].astype(F4)
    layer = total.astype(BF)
    o_ref[...] = layer
    resid = (layer.astype(F4) - t_ref[...].astype(F4)).astype(BF)
    for i in range(m_ref.shape[0]):
        m_ref[i] = resid


def redispatch_body(r_ref, p_ref, m_ref):
    x = jnp.concatenate([r_ref[i] for i in range(r_ref.shape[0])], axis=0)
    for e in range(p_ref.shape[0]):
        m_ref[e] = dot(p_ref[e], x).astype(BF)


def delta_in_body(r_ref, w_ref, out_ref, wd_ref, f_ref, s_ref):
    l, h = w_ref.shape[0], w_ref.shape[1]
    n, fs = f_ref.shape[0], f_ref.shape[1] // 4
    slots = s_ref.shape[0]
    rows, tiles = [], []
    for e in range(l):
        resid = r_ref[e].astype(F4)[: CAP * h]
        out = out_ref[e * CAP * h : (e + 1) * CAP * h]
        column = jnp.sum(resid * out, axis=1, keepdims=True)
        tiles.append(split3(column_tile(column, h), 8))
        rows.append(scale_rows(resid, w_ref[e], h))
    rows.append(jnp.zeros((slots - l * CAP * h, LANES), F4))
    scaled = jnp.concatenate(rows, axis=0).astype(BF)
    s_ref[...] = scaled
    half = l // 2
    packed = roll(jnp.concatenate(tiles[:half], axis=0), 64) + roll(
        jnp.concatenate(tiles[half:], axis=0), 88
    )
    packed = jnp.concatenate([packed, jnp.zeros((fs - packed.shape[0], LANES), F4)], axis=0)
    for d in range(n):
        part = dot(wd_ref[d * fs : (d + 1) * fs], scaled, 1, 1)
        message = blocks_to_rows(part)
        last = message[3 * fs :] + packed
        f_ref[d] = jnp.concatenate([message[: 3 * fs], last], axis=0).astype(BF)


def grad_down_body(h_ref, s_ref, g_ref):
    n, fs = g_ref.shape[0], g_ref.shape[1] // 2
    for d in range(n):
        grad = dot(h_ref[d * fs : (d + 1) * fs], s_ref[...])
        hi = grad.astype(BF)
        g_ref[d, :fs] = hi
        g_ref[d, fs:] = (grad - hi.astype(F4)).astype(BF)


def delta_body(r_ref, gate_ref, up_ref, gd_ref, f_ref, dgu_ref, dot_ref):
    n, fs = f_ref.shape[0], gate_ref.shape[0]
    l, h = dot_ref.shape[0], dot_ref.shape[1]
    total = r_ref[0].astype(F4)
    for i in range(1, n):
        total = total + r_ref[i].astype(F4)
    packed = total[3 * fs : 3 * fs + l * h // 2]
    first, second = join3(roll(packed, -64), 8), join3(roll(packed, -88), 8)
    at = lane((h, LANES))
    for e in range(l):
        source = first if e < l // 2 else second
        i = e % (l // 2)
        dot_ref[e] = jnp.where(at < CAP, source[i * h : (i + 1) * h], 0.0)
    dh = rows_to_blocks(total, fs)
    gate, up = gate_ref[...], up_ref[...]
    s = jax.nn.sigmoid(gate)
    dgate = (dh * up * s * (1.0 + gate * (1.0 - s))).astype(BF)
    dup = (dh * gate * s).astype(BF)
    dgu = jnp.concatenate([dgate, dup], axis=0)
    dgu_ref[...] = dgu
    message = blocks_to_rows(dgu)
    for d in range(n):
        f_ref[d, : 8 * fs] = message
        f_ref[d, 8 * fs :] = gd_ref[d]


def back_body(r_ref, wgu_ref, dot_ref, m_ref):
    n, fs = r_ref.shape[0], r_ref.shape[1] // 10
    l, h = dot_ref.shape[0], dot_ref.shape[1]
    dgu = jnp.concatenate(
        [rows_to_blocks(r_ref[i, : 8 * fs], 2 * fs) for i in range(n)], axis=0
    )
    back = dot(dgu, wgu_ref[...], 0, 0)
    for e in range(l):
        rows = back[e * CAP * h : (e + 1) * CAP * h]
        m_ref[e] = jnp.concatenate([rows, split3(dot_ref[e], 8)], axis=0).astype(BF)


def grad_gate_body(r_ref, dgu_ref, gg_ref, gu_ref):
    n, fs = r_ref.shape[0], gg_ref.shape[0]
    dgu = dgu_ref[...]
    slots = dgu.shape[1]
    pad = jnp.zeros((slots - r_ref.shape[1] + 3 * fs, 2 * LANES), BF)
    for i in range(n // 2):
        x = jnp.concatenate([r_ref[2 * i, 3 * fs :], r_ref[2 * i + 1, 3 * fs :]], axis=1)
        grad = dot(dgu, jnp.concatenate([x, pad], axis=0))
        part = pl.ds(2 * i * LANES, 2 * LANES)
        gg_ref[:, part] = grad[:fs]
        gu_ref[:, part] = grad[fs:]


def grad_down_out_body(r_ref, gd_ref):
    fs = gd_ref.shape[0]
    for i in range(r_ref.shape[0]):
        hi, mid = r_ref[i, 8 * fs : 9 * fs], r_ref[i, 9 * fs :]
        gd_ref[:, i * LANES : (i + 1) * LANES] = hi.astype(F4) + mid.astype(F4)


def combine_back_body(base_ref, r_ref, p_ref, ids_ref, m_ref):
    l, hosts = r_ref.shape[0], m_ref.shape[0]
    h = hosts
    g = 32
    per = LANES // g
    x = jnp.concatenate([r_ref[i] for i in range(l)], axis=0)
    p = jnp.concatenate([p_ref[i] for i in range(l)], axis=0)
    y = dot(p, x, 0, 0)
    ids = ids_ref[...]
    routes = jnp.zeros(ids.shape, F4)
    for e in range(l):
        tile = join3(r_ref[e].astype(F4)[CAP * h :], 8)
        place = p_ref[e].astype(F4)
        acc = jnp.zeros((h, ids.shape[1]), F4)
        for c in range(CAP):
            acc = acc + place[c * h : (c + 1) * h] * tile[:, c : c + 1]
        at_token = jnp.sum(acc, axis=0, keepdims=True)
        mine = (base_ref[0] + e).astype(F4)
        routes = routes + jnp.where(ids == mine, at_token, 0.0)
    at = lane((8, LANES))
    for i in range(hosts):
        q = i // per
        own = roll(routes[:, q * LANES : (q + 1) * LANES], -(i % per) * g)
        own = split3(jnp.where(at < g, own, 0.0), g)
        m_ref[i] = jnp.concatenate(
            [y[i * g : (i + 1) * g], own, jnp.zeros((8, LANES), F4)], axis=0
        ).astype(BF)


def finish_body(r_ref, t_ref, g_ref):
    total = r_ref[0].astype(F4)
    for i in range(1, r_ref.shape[0]):
        total = total + r_ref[i].astype(F4)
    rows = t_ref.shape[0]
    t_ref[...] = total[:rows].astype(BF)
    g_ref[...] = join3(total[rows : rows + 8], rows)


def exchange(x, axis):
    return lax.all_to_all(x, axis, split_axis=0, concat_axis=0, tiled=True)


def shards(tokens, target, expert_ids, route_weights, w_gate, w_up, w_down):
    h, l, n = lax.axis_size("eh"), lax.axis_size("el"), lax.axis_size("fsdp")
    g, k = expert_ids.shape
    fs, d = w_gate.shape[1], w_gate.shape[2]
    df = tokens.shape[1]
    mean_load = k * g // (h * l)
    assert df == LANES and g == 32 and k == 8 and h % 8 == 0
    assert min(g, mean_load + mean_load // 2 + 1) == CAP
    wg, wu, wd = w_gate[0], w_up[0], w_down[0]
    held, slots = CAP * h * l, 8 * h * l
    base = (lax.axis_index("eh") * l).astype(jnp.int32).reshape(1)

    weights = route_weights.T
    hi = lax.reduce_precision(weights, 8, 7)
    mid = lax.reduce_precision(weights - hi, 8, 7)
    low = weights - hi - mid
    meta = jnp.concatenate([expert_ids.T.astype(F4), hi, mid, low], axis=1).astype(BF)
    first = jnp.concatenate([tokens, meta, jnp.zeros((8, LANES), BF)], axis=0)
    first = jnp.broadcast_to(first[None], (h,) + first.shape)
    got = exchange(first, "eh")
    message, place, ids = call(
        dispatch_body,
        [((l, 8 * h, df), BF), ((l, 8 * h, h * g), BF), ((8, h * g), F4)],
        base, got, smem=(0,), name="dispatch",
    )
    got = exchange(message, "el")
    message, w_tile = call(
        expert_in_body,
        [((n, 3 * fs + held, df), BF), ((l, h, LANES), F4)],
        got, wg, wu, wd, name="expert_in",
    )
    rows = exchange(message, "fsdp")
    gate, up, message = call(
        hidden_body,
        [((fs, slots), F4), ((fs, slots), F4), ((n, fs * slots // LANES, LANES), BF)],
        rows, wg, wu, name="hidden",
    )
    wgu_f = rows[:, : 2 * fs].reshape(n * 2 * fs, df)
    wd_f = rows[:, 2 * fs : 3 * fs].reshape(n * fs, df)
    got = exchange(message, "fsdp")
    out, hidden, message = call(
        expert_out_body,
        [((slots, df), F4), ((n * fs, slots), BF), ((l, 8 * h, df), BF)],
        got, wd_f, w_tile, name="expert_out",
    )
    got = exchange(message, "el")
    (message,) = call(combine_body, [((h, g, df), BF)], got, place, name="combine")
    got = exchange(message, "eh")
    layer_out, message = call(
        resid_body, [((g, df), BF), ((h, g, df), BF)], got, target, name="resid"
    )
    got = exchange(message, "eh")
    (message,) = call(
        redispatch_body, [((l, 8 * h, df), BF)], got, place, name="redispatch"
    )
    got = exchange(message, "el")
    message, scaled = call(
        delta_in_body,
        [((n, fs * slots // LANES, LANES), BF), ((slots, df), BF)],
        got, w_tile, out, wd_f, name="delta_in",
    )
    got = exchange(message, "fsdp")
    (grad_down_parts,) = call(
        grad_down_body, [((n, 2 * fs, df), BF)], hidden, scaled, name="grad_down"
    )
    message, dgu, dots = call(
        delta_body,
        [((n, 10 * fs, LANES), BF), ((2 * fs, slots), BF), ((l, h, LANES), F4)],
        got, gate, up, grad_down_parts, name="delta",
    )
    deltas = exchange(message, "fsdp")
    grad_gate, grad_up = call(
        grad_gate_body, [((fs, d), F4), ((fs, d), F4)], rows, dgu, name="grad_gate"
    )
    (message,) = call(
        back_body, [((l, 8 * h, df), BF)], deltas, wgu_f, dots, name="back"
    )
    got = exchange(message, "el")
    (grad_down,) = call(grad_down_out_body, [((fs, d), F4)], deltas, name="grad_down_out")
    (message,) = call(
        combine_back_body, [((h, g + 16, df), BF)],
        base, got, place, ids, smem=(0,), name="combine_back",
    )
    got = exchange(message, "eh")
    grad_tokens, grad_route = call(
        finish_body, [((g, df), BF), ((8, LANES), F4)], got, name="finish"
    )
    grad_route = grad_route[:, :g].T
    return (layer_out, grad_tokens, grad_route, grad_gate[None], grad_up[None], grad_down[None])


def solution(mesh):
    experts, fsdp = mesh.devices.shape
    split = Mesh(mesh.devices.reshape(HI, experts // HI, fsdp), ("eh", "el", "fsdp"))
    e = ("eh", "el")
    return jax.shard_map(
        shards,
        mesh=split,
        in_specs=(
            P(e, "fsdp"),
            P(e, "fsdp"),
            P(e, None),
            P(e, None),
            P(e, "fsdp", None),
            P(e, "fsdp", None),
            P(e, "fsdp", None),
        ),
        out_specs=(
            P(e, "fsdp"),
            P(e, "fsdp"),
            P(e, None),
            P(e, "fsdp", None),
            P(e, "fsdp", None),
            P(e, "fsdp", None),
        ),
        check_vma=False,
    )
```

```python
import functools

import jax
import jax.numpy as jnp
from jax import lax
from jax.experimental import pallas as pl
from jax.experimental.pallas import tpu as pltpu
from jax.sharding import Mesh, PartitionSpec as P

BF = jnp.bfloat16
F4 = jnp.float32
LANES = 128
HI = 8
CAP = 7


def dot(a, b, ca=1, cb=0):
    return lax.dot_general(a, b, (((ca,), (cb,)), ((), ())), preferred_element_type=F4)


def call(body, outs, *args, smem=(), hbm=(), scratch=(), vmem_mib=16, name=None):
    specs = [
        pl.BlockSpec(
            memory_space=pltpu.SMEM if i in smem else pltpu.HBM if i in hbm else pltpu.VMEM
        )
        for i in range(len(args))
    ]
    nbytes = sum(a.size * a.dtype.itemsize for a in args)
    shapes = [jax.ShapeDtypeStruct(s, d) for s, d in outs]
    return pl.pallas_call(
        body,
        out_shape=shapes,
        in_specs=specs,
        out_specs=[pl.BlockSpec(memory_space=pltpu.VMEM) for _ in shapes],
        scratch_shapes=list(scratch),
        compiler_params=pltpu.CompilerParams(vmem_limit_bytes=vmem_mib * 1024 * 1024),
        cost_estimate=pl.CostEstimate(
            flops=100_000_000, bytes_accessed=int(nbytes), transcendentals=0
        ),
        name=name,
    )(*args)


def lane(shape):
    return lax.broadcasted_iota(jnp.int32, shape, 1)


def roll(x, by):
    by = by % LANES
    return x if by == 0 else pltpu.roll(x, by, 1)


def split3(x, step):
    hi = x.astype(BF).astype(F4)
    rest = x - hi
    mid = rest.astype(BF).astype(F4)
    return hi + roll(mid, step) + roll(rest - mid, 2 * step)


def join3(x, step):
    return x + roll(x, -step) + roll(x, -2 * step)


def column_tile(column, h):
    at = lane((h, LANES))
    tile = jnp.zeros((h, LANES), F4)
    for c in range(CAP):
        tile = jnp.where(at == c, column[c * h : (c + 1) * h], tile)
    return tile


def scale_rows(rows, tile, h):
    return jnp.concatenate(
        [rows[c * h : (c + 1) * h] * tile[:, c : c + 1] for c in range(CAP)], axis=0
    )


def blocks_to_rows(x):
    return jnp.concatenate(
        [x[:, i * LANES : (i + 1) * LANES] for i in range(x.shape[1] // LANES)], axis=0
    )


def rows_to_blocks(x, rows):
    return jnp.concatenate(
        [x[i * rows : (i + 1) * rows] for i in range(x.shape[0] // rows)], axis=1
    )


def first_body(base_ref, ids_in, weights_in, t_in, m_ref, ids_ref, weights_ref, t_ref, sem):
    k, g = ids_ref.shape
    pairs = ((ids_in, ids_ref), (weights_in, weights_ref), (t_in, t_ref))
    copies = [pltpu.make_async_copy(a, b, sem.at[i]) for i, (a, b) in enumerate(pairs)]
    for copy in copies:
        copy.start()
    for copy in copies:
        copy.wait()
    w = weights_ref[...]
    hi = w.astype(BF)
    rest = w - hi.astype(F4)
    mid = rest.astype(BF)
    low = (rest - mid.astype(F4)).astype(BF)
    row = lax.broadcasted_iota(jnp.int32, (g, LANES), 0)
    col = lane((g, LANES))
    meta = jnp.zeros((k, LANES), F4)
    for i, part in enumerate((ids_ref[...].astype(F4).astype(BF), hi, mid, low)):
        move = jnp.where(col == row + i * g, 1.0, 0.0).astype(BF)
        meta = meta + dot(part, move)
    tail = jnp.concatenate([meta, jnp.zeros_like(meta)], axis=0).astype(BF)
    message = jnp.concatenate([t_ref[...], tail], axis=0)
    for i in range(m_ref.shape[0]):
        m_ref[i] = message


def weights_body(wg_ref, wu_ref, wd_ref, wgu_ref, wd_out_ref):
    fs = wg_ref.shape[0]
    wgu_ref[:fs] = wg_ref[...]
    wgu_ref[fs:] = wu_ref[...]
    wd_out_ref[...] = wd_ref[...]


def dispatch_body(base_ref, r_ref, m_ref, p_ref, ids_ref):
    h, l = r_ref.shape[0], m_ref.shape[0]
    g = 32
    width = h * g
    per = LANES // g
    at = lane((8, LANES))
    metas = [r_ref[i].astype(F4)[g : g + 8] for i in range(h)]

    def gathered(parts, start):
        out = []
        for q in range(h // per):
            acc = jnp.zeros((8, LANES), F4)
            for i in range(per):
                moved = roll(parts[q * per + i], i * g - start)
                acc = jnp.where(at // g == i, moved, acc)
            out.append(acc)
        return jnp.concatenate(out, axis=1)

    ids = gathered(metas, 0)
    weights = gathered([join3(m, g) for m in metas], g)
    ids_ref[...] = ids
    mine = (lax.broadcasted_iota(jnp.int32, (l, width), 0) + base_ref[0]).astype(F4)
    named = jnp.zeros((l, width), F4)
    weight_at = jnp.zeros((l, width), F4)
    for k in range(8):
        hit = ids[k : k + 1] == mine
        named = named + jnp.where(hit, 1.0, 0.0)
        weight_at = weight_at + jnp.where(hit, weights[k : k + 1], 0.0)
    row = lax.broadcasted_iota(jnp.int32, (width, width), 0)
    col = lane((width, width))
    before = jnp.where((row // g == col // g) & (row < col), 1.0, 0.0).astype(BF)
    rank = dot(named.astype(BF), before)
    rank = jnp.where(named > 0.0, rank, -1.0)
    block = lane((h, width)) // g == lax.broadcasted_iota(jnp.int32, (h, width), 0)
    x = jnp.concatenate([r_ref[i][:g] for i in range(h)], axis=0)
    for e in range(l):
        own = jnp.broadcast_to(rank[e : e + 1], (h, width))
        place = jnp.concatenate(
            [jnp.where(block & (own == float(c)), 1.0, 0.0) for c in range(8)], axis=0
        )
        column = jnp.sum(place * weight_at[e : e + 1], axis=1, keepdims=True)
        place = place.astype(BF)
        p_ref[e] = place
        rows = dot(place, x)
        tile = split3(column_tile(column, h), 8)
        m_ref[e] = jnp.concatenate([rows[: CAP * h], tile], axis=0).astype(BF)


def expert_in_body(r_ref, wd_ref, f_ref, w_ref):
    l, h = r_ref.shape[0], r_ref.shape[1] // 8
    fs = wd_ref.shape[0]
    rows = []
    for e in range(l):
        v = r_ref[e].astype(F4)
        rows.append(v[: CAP * h])
        w_ref[e] = join3(v[CAP * h :], 8)
    x = jnp.concatenate(rows, axis=0).astype(BF)
    for d in range(f_ref.shape[0]):
        f_ref[d, :fs] = wd_ref[:, d * LANES : (d + 1) * LANES]
        f_ref[d, fs:] = x


def hidden_body(r_ref, wgu_ref, gate_ref, up_ref, wd_ref, f_ref):
    n, fs = r_ref.shape[0], gate_ref.shape[0]
    slots = gate_ref.shape[1]
    held = r_ref.shape[1] - fs
    pad = jnp.zeros((slots - held, 2 * LANES), BF)
    total = jnp.zeros((2 * fs, slots), F4)
    for i in range(n // 2):
        x = jnp.concatenate([r_ref[2 * i, fs:], r_ref[2 * i + 1, fs:]], axis=1)
        x = jnp.concatenate([x, pad], axis=0)
        w = wgu_ref[:, 2 * i * LANES : 2 * (i + 1) * LANES]
        total = total + dot(w, x, 1, 1)
    gate, up = total[:fs], total[fs:]
    gate_ref[...] = gate
    up_ref[...] = up
    hidden = (gate * jax.nn.sigmoid(gate) * up).astype(BF)
    message = blocks_to_rows(hidden)
    for d in range(n):
        f_ref[d] = message
        wd_ref[d * fs : (d + 1) * fs] = r_ref[d, :fs]


def expert_out_body(r_ref, wd_ref, w_ref, out_ref, h_ref, m_ref):
    n, fs = r_ref.shape[0], r_ref.shape[1] // 4
    l, h = w_ref.shape[0], w_ref.shape[1]
    hidden = jnp.concatenate([rows_to_blocks(r_ref[i], fs) for i in range(n)], axis=0)
    h_ref[...] = hidden
    out = dot(hidden, wd_ref[...], 0, 0)
    out_ref[...] = out
    for e in range(l):
        rows = out[e * CAP * h : (e + 1) * CAP * h]
        rows = scale_rows(rows, w_ref[e], h)
        m_ref[e] = jnp.concatenate([rows, jnp.zeros((h, LANES), F4)], axis=0).astype(BF)


def combine_body(r_ref, p_ref, m_ref):
    l, rows = r_ref.shape[0], r_ref.shape[1]
    x = jnp.concatenate([r_ref[i] for i in range(l)], axis=0)
    p = jnp.concatenate([p_ref[i] for i in range(l)], axis=0)
    y = dot(p, x, 0, 0).astype(BF)
    g = m_ref.shape[1]
    for i in range(m_ref.shape[0]):
        m_ref[i] = y[i * g : (i + 1) * g]


def resid_body(r_ref, t_ref, o_ref, m_ref):
    total = r_ref[0].astype(F4)
    for i in range(1, r_ref.shape[0]):
        total = total + r_ref[i].astype(F4)
    layer = total.astype(BF)
    o_ref[...] = layer
    resid = (layer.astype(F4) - t_ref[...].astype(F4)).astype(BF)
    for i in range(m_ref.shape[0]):
        m_ref[i] = resid


def redispatch_body(r_ref, p_ref, m_ref):
    x = jnp.concatenate([r_ref[i] for i in range(r_ref.shape[0])], axis=0)
    for e in range(p_ref.shape[0]):
        m_ref[e] = dot(p_ref[e], x).astype(BF)


def delta_in_body(r_ref, w_ref, out_ref, wd_ref, h_ref, f_ref, g_ref):
    l, h = w_ref.shape[0], w_ref.shape[1]
    n, fs = f_ref.shape[0], f_ref.shape[1] // 4
    slots = h_ref.shape[1]
    rows, tiles = [], []
    for e in range(l):
        resid = r_ref[e].astype(F4)[: CAP * h]
        out = out_ref[e * CAP * h : (e + 1) * CAP * h]
        column = jnp.sum(resid * out, axis=1, keepdims=True)
        tiles.append(split3(column_tile(column, h), 8))
        rows.append(scale_rows(resid, w_ref[e], h))
    rows.append(jnp.zeros((slots - l * CAP * h, LANES), F4))
    scaled = jnp.concatenate(rows, axis=0).astype(BF)
    half = l // 2
    packed = roll(jnp.concatenate(tiles[:half], axis=0), 64) + roll(
        jnp.concatenate(tiles[half:], axis=0), 88
    )
    packed = jnp.concatenate([packed, jnp.zeros((fs - packed.shape[0], LANES), F4)], axis=0)
    for d in range(n):
        part = dot(wd_ref[d * fs : (d + 1) * fs], scaled, 1, 1)
        message = blocks_to_rows(part)
        last = message[3 * fs :] + packed
        f_ref[d] = jnp.concatenate([message[: 3 * fs], last], axis=0).astype(BF)
        g_ref[d] = dot(h_ref[d * fs : (d + 1) * fs], scaled).astype(BF)


def delta_body(r_ref, gate_ref, up_ref, wgu_ref, gd_ref, f_ref, dgu_ref, dot_ref):
    n, fs = f_ref.shape[0], gate_ref.shape[0]
    l, h = dot_ref.shape[0], dot_ref.shape[1]
    total = r_ref[0].astype(F4)
    for i in range(1, n):
        total = total + r_ref[i].astype(F4)
    packed = total[3 * fs : 3 * fs + l * h // 2]
    first, second = join3(roll(packed, -64), 8), join3(roll(packed, -88), 8)
    at = lane((h, LANES))
    for e in range(l):
        source = first if e < l // 2 else second
        i = e % (l // 2)
        dot_ref[e] = jnp.where(at < CAP, source[i * h : (i + 1) * h], 0.0)
    dh = rows_to_blocks(total, fs)
    gate, up = gate_ref[...], up_ref[...]
    s = jax.nn.sigmoid(gate)
    dgate = (dh * up * s * (1.0 + gate * (1.0 - s))).astype(BF)
    dup = (dh * gate * s).astype(BF)
    dgu = jnp.concatenate([dgate, dup], axis=0)
    dgu_ref[...] = dgu
    held = CAP * h * l
    for i in range(n // 2):
        back = dot(dgu, wgu_ref[:, 2 * i * LANES : 2 * (i + 1) * LANES], 0, 0)
        back = back[:held].astype(BF)
        for d in (2 * i, 2 * i + 1):
            own = (d - 2 * i) * LANES
            f_ref[d, :fs] = gd_ref[d]
            f_ref[d, fs:] = back[:, own : own + LANES]


def back_body(r_ref, dot_ref, m_ref, gd_ref):
    l, h = dot_ref.shape[0], dot_ref.shape[1]
    fs = r_ref.shape[1] - CAP * h * l
    for e in range(l):
        part = pl.ds(fs + e * CAP * h, CAP * h)
        rows = r_ref[0, part].astype(F4)
        for i in range(1, r_ref.shape[0]):
            rows = rows + r_ref[i, part].astype(F4)
        m_ref[e] = jnp.concatenate([rows, split3(dot_ref[e], 8)], axis=0).astype(BF)
    for i in range(r_ref.shape[0]):
        gd_ref[:, i * LANES : (i + 1) * LANES] = r_ref[i, :fs].astype(F4)


def grads_body(tick_ref, x_ref, dgu_ref, gg_ref, gu_ref):
    n, fs = x_ref.shape[0], gg_ref.shape[0]
    dgu = dgu_ref[...]
    pad = jnp.zeros((dgu.shape[1] - x_ref.shape[1] + fs, 2 * LANES), BF)
    for i in range(n // 2):
        x = jnp.concatenate([x_ref[2 * i, fs:], x_ref[2 * i + 1, fs:]], axis=1)
        grad = dot(dgu, jnp.concatenate([x, pad], axis=0))
        part = pl.ds(2 * i * LANES, 2 * LANES)
        gg_ref[:, part] = grad[:fs]
        gu_ref[:, part] = grad[fs:]


def combine_back_body(base_ref, r_ref, p_ref, ids_ref, m_ref, tick_ref):
    l, hosts = r_ref.shape[0], m_ref.shape[0]
    h = hosts
    g = 32
    per = LANES // g
    x = jnp.concatenate([r_ref[i] for i in range(l)], axis=0)
    p = jnp.concatenate([p_ref[i] for i in range(l)], axis=0)
    y = dot(p, x, 0, 0)
    ids = ids_ref[...]
    tick_ref[...] = ids[:, :LANES]
    routes = jnp.zeros(ids.shape, F4)
    for e in range(l):
        tile = join3(r_ref[e].astype(F4)[CAP * h :], 8)
        place = p_ref[e].astype(F4)
        acc = jnp.zeros((h, ids.shape[1]), F4)
        for c in range(CAP):
            acc = acc + place[c * h : (c + 1) * h] * tile[:, c : c + 1]
        at_token = jnp.sum(acc, axis=0, keepdims=True)
        mine = (base_ref[0] + e).astype(F4)
        routes = routes + jnp.where(ids == mine, at_token, 0.0)
    at = lane((8, LANES))
    for i in range(hosts):
        q = i // per
        own = roll(routes[:, q * LANES : (q + 1) * LANES], -(i % per) * g)
        own = split3(jnp.where(at < g, own, 0.0), g)
        m_ref[i] = jnp.concatenate(
            [y[i * g : (i + 1) * g], own, jnp.zeros((8, LANES), F4)], axis=0
        ).astype(BF)


def finish_body(r_ref, t_ref, g_ref):
    total = r_ref[0].astype(F4)
    for i in range(1, r_ref.shape[0]):
        total = total + r_ref[i].astype(F4)
    rows = t_ref.shape[0]
    t_ref[...] = total[:rows].astype(BF)
    g_ref[...] = join3(total[rows : rows + 8], rows)[:, :rows]


def exchange(x, axis):
    return lax.all_to_all(x, axis, split_axis=0, concat_axis=0, tiled=True)


def shards(tokens, target, expert_ids, route_weights, w_gate, w_up, w_down):
    h, l, n = lax.axis_size("eh"), lax.axis_size("el"), lax.axis_size("fsdp")
    g, k = expert_ids.shape
    fs, d = w_gate.shape[1], w_gate.shape[2]
    df = tokens.shape[1]
    mean_load = k * g // (h * l)
    assert df == LANES and g == 32 and k == 8 and h % 8 == 0
    assert min(g, mean_load + mean_load // 2 + 1) == CAP
    wg, wu, wd = w_gate[0], w_up[0], w_down[0]
    held, slots = CAP * h * l, 8 * h * l
    base = (lax.axis_index("eh") * l).astype(jnp.int32).reshape(1)

    (message,) = call(
        first_body, [((h, g + 16, df), BF)],
        base, expert_ids.T, route_weights.T, tokens, smem=(0,), hbm=(1, 2, 3),
        scratch=(
            pltpu.VMEM((k, g), jnp.int32), pltpu.VMEM((k, g), F4), pltpu.VMEM((g, df), BF),
            pltpu.SemaphoreType.DMA((3,)),
        ),
        vmem_mib=60, name="first",
    )
    got = exchange(message, "eh")
    wgu, wd = call(
        weights_body, [((2 * fs, d), BF), ((fs, d), BF)], wg, wu, wd, name="weights"
    )
    message, place, ids = call(
        dispatch_body,
        [((l, 8 * h, df), BF), ((l, 8 * h, h * g), BF), ((8, h * g), F4)],
        base, got, smem=(0,), name="dispatch",
    )
    got = exchange(message, "el")
    message, w_tile = call(
        expert_in_body,
        [((n, fs + held, df), BF), ((l, h, LANES), F4)],
        got, wd, name="expert_in",
    )
    rows = exchange(message, "fsdp")
    packed = (n, fs * slots // LANES, LANES)
    gate, up, wd_f, message = call(
        hidden_body,
        [((fs, slots), F4), ((fs, slots), F4), ((n * fs, df), BF), (packed, BF)],
        rows, wgu, name="hidden",
    )
    got = exchange(message, "fsdp")
    out, hidden, message = call(
        expert_out_body,
        [((slots, df), F4), ((n * fs, slots), BF), ((l, 8 * h, df), BF)],
        got, wd_f, w_tile, name="expert_out",
    )
    got = exchange(message, "el")
    (message,) = call(combine_body, [((h, g, df), BF)], got, place, name="combine")
    got = exchange(message, "eh")
    layer_out, message = call(
        resid_body, [((g, df), BF), ((h, g, df), BF)], got, target, name="resid"
    )
    got = exchange(message, "eh")
    (message,) = call(
        redispatch_body, [((l, 8 * h, df), BF)], got, place, name="redispatch"
    )
    got = exchange(message, "el")
    message, down = call(
        delta_in_body,
        [(packed, BF), ((n, fs, df), BF)],
        got, w_tile, out, wd_f, hidden, name="delta_in",
    )
    got = exchange(message, "fsdp")
    message, dgu, dots = call(
        delta_body,
        [((n, fs + held, df), BF), ((2 * fs, slots), BF), ((l, h, LANES), F4)],
        got, gate, up, wgu, down, name="delta",
    )
    got = exchange(message, "fsdp")
    message, grad_down = call(
        back_body, [((l, 8 * h, df), BF), ((fs, d), F4)], got, dots, name="back"
    )
    got = exchange(message, "el")
    message, tick = call(
        combine_back_body,
        [((h, g + 16, df), BF), ((8, LANES), F4)],
        base, got, place, ids, smem=(0,), name="combine_back",
    )
    got = exchange(message, "eh")
    grad_gate, grad_up = call(
        grads_body, [((fs, d), F4)] * 2, tick, rows, dgu, name="grads"
    )
    grad_tokens, grad_route = call(
        finish_body, [((g, df), BF), ((8, g), F4)], got, name="finish"
    )
    return (
        layer_out, grad_tokens, grad_route.T, grad_gate[None], grad_up[None], grad_down[None]
    )


def solution(mesh):
    experts, fsdp = mesh.devices.shape
    split = Mesh(mesh.devices.reshape(HI, experts // HI, fsdp), ("eh", "el", "fsdp"))
    e = ("eh", "el")
    return jax.shard_map(
        shards,
        mesh=split,
        in_specs=(
            P(e, "fsdp"),
            P(e, "fsdp"),
            P(e, None),
            P(e, None),
            P(e, "fsdp", None),
            P(e, "fsdp", None),
            P(e, "fsdp", None),
        ),
        out_specs=(
            P(e, "fsdp"),
            P(e, "fsdp"),
            P(e, None),
            P(e, "fsdp", None),
            P(e, "fsdp", None),
            P(e, "fsdp", None),
        ),
        check_vma=False,
    )
```

```python
import functools

import jax
import jax.numpy as jnp
from jax import lax
from jax.experimental import pallas as pl
from jax.experimental.pallas import tpu as pltpu
from jax.sharding import Mesh, PartitionSpec as P

BF = jnp.bfloat16
F4 = jnp.float32
LANES = 128
NEAR = 4
CAP = 7
ROWS = 8 * NEAR
HELD = CAP * NEAR


def dot(a, b, ca=1, cb=0):
    return lax.dot_general(a, b, (((ca,), (cb,)), ((), ())), preferred_element_type=F4)


def call(body, outs, *args, smem=(), hbm=(), scratch=(), vmem_mib=16, name=None):
    specs = [
        pl.BlockSpec(
            memory_space=pltpu.SMEM if i in smem else pltpu.HBM if i in hbm else pltpu.VMEM
        )
        for i in range(len(args))
    ]
    nbytes = sum(a.size * a.dtype.itemsize for a in args)
    shapes = [jax.ShapeDtypeStruct(s, d) for s, d in outs]
    return pl.pallas_call(
        body,
        out_shape=shapes,
        in_specs=specs,
        out_specs=[pl.BlockSpec(memory_space=pltpu.VMEM) for _ in shapes],
        scratch_shapes=list(scratch),
        compiler_params=pltpu.CompilerParams(vmem_limit_bytes=vmem_mib * 1024 * 1024),
        cost_estimate=pl.CostEstimate(
            flops=100_000_000, bytes_accessed=int(nbytes), transcendentals=0
        ),
        name=name,
    )(*args)


def lane(shape):
    return lax.broadcasted_iota(jnp.int32, shape, 1)


def roll(x, by):
    by = by % LANES
    return x if by == 0 else pltpu.roll(x, by, 1)


def split3(x, step):
    hi = x.astype(BF).astype(F4)
    rest = x - hi
    mid = rest.astype(BF).astype(F4)
    return hi + roll(mid, step) + roll(rest - mid, 2 * step)


def join3(x, step):
    return x + roll(x, -step) + roll(x, -2 * step)


def index(shape):
    return lax.broadcasted_iota(jnp.int32, shape, 0), lane(shape)


def onehot(hit):
    return jnp.where(hit, 1.0, 0.0).astype(BF)


def to_slots():
    i, j = index((2 * HELD, 2 * ROWS))
    return onehot(j == i // HELD * ROWS + i % HELD)


def to_message():
    i, j = index((2 * ROWS, 2 * HELD))
    return onehot((j == i // ROWS * HELD + i % ROWS) & (i % ROWS < HELD))


def scalar_rows():
    i, j = index((2 * HELD, 2 * ROWS))
    return onehot(j == i // HELD * ROWS + HELD + i % HELD % NEAR)


def scalars_to_tile():
    i, j = index((2 * NEAR, 2 * HELD))
    return onehot((j // HELD == i // NEAR) & (j % HELD % NEAR == i % NEAR))


def tile_to_message():
    i, j = index((2 * ROWS, 2 * NEAR))
    return onehot((i % ROWS >= HELD) & (j == i // ROWS * NEAR + i % ROWS - HELD))


def spread(column, held):
    i, j = index((column.shape[0], LANES))
    return split3(jnp.where(j == i % held // NEAR, column, 0.0), 8).astype(BF)


def gathered_column(rows, held):
    i, j = index(rows.shape)
    mine = (j % 8 == i % held // NEAR) & (j < 24)
    return jnp.sum(jnp.where(mine, rows, 0.0), axis=1, keepdims=True)


def pair(ref, p):
    return jnp.concatenate([ref[2 * p], ref[2 * p + 1]], axis=0)


def blocks_to_rows(x):
    return jnp.concatenate(
        [x[:, i * LANES : (i + 1) * LANES] for i in range(x.shape[1] // LANES)], axis=0
    )


def rows_to_blocks(x, rows):
    return jnp.concatenate(
        [x[i * rows : (i + 1) * rows] for i in range(x.shape[0] // rows)], axis=1
    )


def first_body(base_ref, ids_in, weights_in, t_in, m_ref, ids_ref, weights_ref, t_ref, sem):
    k, g = ids_ref.shape
    pairs = ((ids_in, ids_ref), (weights_in, weights_ref), (t_in, t_ref))
    copies = [pltpu.make_async_copy(a, b, sem.at[i]) for i, (a, b) in enumerate(pairs)]
    for copy in copies:
        copy.start()
    for copy in copies:
        copy.wait()
    w = weights_ref[...]
    hi = w.astype(BF)
    rest = w - hi.astype(F4)
    mid = rest.astype(BF)
    low = (rest - mid.astype(F4)).astype(BF)
    row = lax.broadcasted_iota(jnp.int32, (g, LANES), 0)
    col = lane((g, LANES))
    meta = jnp.zeros((k, LANES), F4)
    for i, part in enumerate((ids_ref[...].astype(F4).astype(BF), hi, mid, low)):
        move = jnp.where(col == row + i * g, 1.0, 0.0).astype(BF)
        meta = meta + dot(part, move)
    tail = jnp.concatenate([meta, jnp.zeros_like(meta)], axis=0).astype(BF)
    message = jnp.concatenate([t_ref[...], tail], axis=0)
    for i in range(m_ref.shape[0]):
        m_ref[i] = message


def weights_body(wg_ref, wu_ref, wd_ref, wgu_ref, wd_out_ref):
    fs = wg_ref.shape[0]
    wgu_ref[:fs] = wg_ref[...]
    wgu_ref[fs:] = wu_ref[...]
    wd_out_ref[...] = wd_ref[...]


def dispatch_body(base_ref, r_ref, m_ref, p_ref, ids_ref):
    l, h = r_ref.shape[0], m_ref.shape[0]
    g = LANES // l
    at = lane((8, LANES))
    metas = [r_ref[i].astype(F4)[g : g + 8] for i in range(l)]

    def gathered(parts, start):
        out = jnp.zeros((8, LANES), F4)
        for i in range(l):
            out = jnp.where(at // g == i, roll(parts[i], i * g - start), out)
        return out

    ids = gathered(metas, 0)
    weights = gathered([join3(m, g) for m in metas], g)
    ids_ref[...] = ids
    mine = (lax.broadcasted_iota(jnp.int32, (h, LANES), 0) * l + base_ref[0]).astype(F4)
    named = jnp.zeros((h, LANES), F4)
    weight_at = jnp.zeros((h, LANES), F4)
    for k in range(8):
        hit = ids[k : k + 1] == mine
        named = named + jnp.where(hit, 1.0, 0.0)
        weight_at = weight_at + jnp.where(hit, weights[k : k + 1], 0.0)
    row, col = index((LANES, LANES))
    rank = dot(named.astype(BF), onehot((row // g == col // g) & (row < col)))
    rank = jnp.where(named > 0.0, rank, -1.0)
    x = jnp.concatenate([r_ref[i][:g] for i in range(l)], axis=0)
    i, j = index((ROWS, LANES))
    own = (j // g == i % NEAR) & (i < HELD)
    slot = (i // NEAR).astype(F4)
    i, j = index((ROWS, ROWS))
    down = onehot((i >= HELD) & (j % NEAR == i - HELD) & (j < HELD))
    for e in range(h):
        place = jnp.where(own & (rank[e : e + 1] == slot), 1.0, 0.0)
        column = jnp.sum(place * weight_at[e : e + 1], axis=1, keepdims=True)
        place = place.astype(BF)
        p_ref[e] = place
        m_ref[e] = (dot(place, x) + dot(down, spread(column, ROWS))).astype(BF)


def expert_in_body(r_ref, wd_ref, f_ref, w_ref):
    fs = wd_ref.shape[0]
    slots, scalars = to_slots(), scalar_rows()
    rows = []
    for p in range(r_ref.shape[0] // 2):
        v = pair(r_ref, p)
        rows.append(dot(slots, v))
        column = gathered_column(dot(scalars, v), HELD)
        w_ref[p] = jnp.broadcast_to(column, (2 * HELD, LANES))
    x = jnp.concatenate(rows, axis=0).astype(BF)
    for d in range(f_ref.shape[0]):
        f_ref[d, :fs] = wd_ref[:, d * LANES : (d + 1) * LANES]
        f_ref[d, fs:] = x


def hidden_body(r_ref, wgu_ref, gate_ref, up_ref, wd_ref, f_ref):
    n, fs = r_ref.shape[0], gate_ref.shape[0]
    slots = gate_ref.shape[1]
    held = r_ref.shape[1] - fs
    pad = jnp.zeros((slots - held, 2 * LANES), BF)
    total = jnp.zeros((2 * fs, slots), F4)
    for i in range(n // 2):
        x = jnp.concatenate([r_ref[2 * i, fs:], r_ref[2 * i + 1, fs:]], axis=1)
        x = jnp.concatenate([x, pad], axis=0)
        w = wgu_ref[:, 2 * i * LANES : 2 * (i + 1) * LANES]
        total = total + dot(w, x, 1, 1)
    gate, up = total[:fs], total[fs:]
    gate_ref[...] = gate
    up_ref[...] = up
    hidden = (gate * jax.nn.sigmoid(gate) * up).astype(BF)
    message = blocks_to_rows(hidden)
    for d in range(n):
        f_ref[d] = message
        wd_ref[d * fs : (d + 1) * fs] = r_ref[d, :fs]


def expert_out_body(r_ref, wd_ref, w_ref, out_ref, h_ref, m_ref):
    n, fs = r_ref.shape[0], r_ref.shape[1] // 4
    hidden = jnp.concatenate([rows_to_blocks(r_ref[i], fs) for i in range(n)], axis=0)
    h_ref[...] = hidden
    out = dot(hidden, wd_ref[...], 0, 0)
    out_ref[...] = out
    message = to_message()
    for p in range(w_ref.shape[0]):
        rows = out[2 * p * HELD : 2 * (p + 1) * HELD] * w_ref[p]
        rows = dot(message, rows.astype(BF)).astype(BF)
        m_ref[2 * p] = rows[:ROWS]
        m_ref[2 * p + 1] = rows[ROWS:]


def stacked(ref):
    return jnp.concatenate([ref[i] for i in range(ref.shape[0])], axis=0)


def combine_body(r_ref, p_ref, t_ref, m_ref):
    y = dot(stacked(p_ref), stacked(r_ref), 0, 0).astype(BF)
    message = jnp.concatenate([y, t_ref[...]], axis=0)
    for i in range(m_ref.shape[0]):
        m_ref[i] = message


def resid_body(base_ref, r_ref, p_ref, o_ref, m_ref, layer_ref):
    l, g = r_ref.shape[0], o_ref.shape[0]
    total = r_ref[0, : l * g].astype(F4)
    for i in range(1, l):
        total = total + r_ref[i, : l * g].astype(F4)
    layer = total.astype(BF).astype(F4)
    layer_ref[...] = layer
    o_ref[...] = layer_ref[pl.ds(pl.multiple_of(base_ref[0] * g, g), g)].astype(BF)
    target = jnp.concatenate([r_ref[i, l * g :] for i in range(l)], axis=0)
    resid = (layer - target.astype(F4)).astype(BF)
    for e in range(p_ref.shape[0]):
        m_ref[e] = dot(p_ref[e], resid).astype(BF)


def delta_in_body(r_ref, w_ref, out_ref, wd_ref, h_ref, f_ref, g_ref):
    pairs = w_ref.shape[0]
    n, fs = f_ref.shape[0], f_ref.shape[1] // 4
    slots = h_ref.shape[1]
    run = 2 * HELD
    rows, tiles = [], []
    take, tile = to_slots(), scalars_to_tile()
    for p in range(pairs):
        resid = dot(take, pair(r_ref, p))
        column = jnp.sum(resid * out_ref[p * run : (p + 1) * run], axis=1, keepdims=True)
        tiles.append(dot(tile, spread(column, HELD)))
        rows.append(resid * w_ref[p])
    rows.append(jnp.zeros((slots - pairs * run, LANES), F4))
    scaled = jnp.concatenate(rows, axis=0).astype(BF)
    half = pairs // 2
    packed = roll(jnp.concatenate(tiles[:half], axis=0), 64) + roll(
        jnp.concatenate(tiles[half:], axis=0), 88
    )
    packed = jnp.concatenate([packed, jnp.zeros((fs - packed.shape[0], LANES), F4)], axis=0)
    for d in range(n):
        part = dot(wd_ref[d * fs : (d + 1) * fs], scaled, 1, 1)
        message = blocks_to_rows(part)
        last = message[3 * fs :] + packed
        f_ref[d] = jnp.concatenate([message[: 3 * fs], last], axis=0).astype(BF)
        g_ref[d] = dot(h_ref[d * fs : (d + 1) * fs], scaled).astype(BF)


def delta_body(r_ref, gate_ref, up_ref, wgu_ref, gd_ref, f_ref, dgu_ref, dot_ref):
    n, fs = f_ref.shape[0], gate_ref.shape[0]
    l, h = dot_ref.shape[0], dot_ref.shape[1]
    total = r_ref[0].astype(F4)
    for i in range(1, n):
        total = total + r_ref[i].astype(F4)
    packed = total[3 * fs : 3 * fs + l * h // 2]
    first, second = join3(roll(packed, -64), 8), join3(roll(packed, -88), 8)
    at = lane((h, LANES))
    for e in range(l):
        source = first if e < l // 2 else second
        i = e % (l // 2)
        dot_ref[e] = jnp.where(at < CAP, source[i * h : (i + 1) * h], 0.0)
    dh = rows_to_blocks(total, fs)
    gate, up = gate_ref[...], up_ref[...]
    s = jax.nn.sigmoid(gate)
    dgate = (dh * up * s * (1.0 + gate * (1.0 - s))).astype(BF)
    dup = (dh * gate * s).astype(BF)
    dgu = jnp.concatenate([dgate, dup], axis=0)
    dgu_ref[...] = dgu
    held = 2 * HELD * l
    for i in range(n // 2):
        back = dot(dgu, wgu_ref[:, 2 * i * LANES : 2 * (i + 1) * LANES], 0, 0)
        back = back[:held].astype(BF)
        for d in (2 * i, 2 * i + 1):
            own = (d - 2 * i) * LANES
            f_ref[d, :fs] = gd_ref[d]
            f_ref[d, fs:] = back[:, own : own + LANES]


def back_body(r_ref, dot_ref, m_ref, gd_ref, tick_ref):
    pairs = dot_ref.shape[0]
    run = 2 * HELD
    fs = r_ref.shape[1] - run * pairs
    message, scalars = to_message(), tile_to_message()
    for p in range(pairs):
        part = pl.ds(fs + p * run, run)
        rows = r_ref[0, part].astype(F4)
        for i in range(1, r_ref.shape[0]):
            rows = rows + r_ref[i, part].astype(F4)
        rows = dot(message, rows.astype(BF)) + dot(scalars, split3(dot_ref[p], 8).astype(BF))
        rows = rows.astype(BF)
        m_ref[2 * p] = rows[:ROWS]
        m_ref[2 * p + 1] = rows[ROWS:]
    for i in range(r_ref.shape[0]):
        gd_ref[:, i * LANES : (i + 1) * LANES] = r_ref[i, :fs].astype(F4)
    tick_ref[...] = dot_ref[0]


def grads_body(tick_ref, x_ref, dgu_ref, gg_ref, gu_ref):
    n, fs = x_ref.shape[0], gg_ref.shape[0]
    dgu = dgu_ref[...]
    pad = jnp.zeros((dgu.shape[1] - x_ref.shape[1] + fs, 2 * LANES), BF)
    for i in range(n // 2):
        x = jnp.concatenate([x_ref[2 * i, fs:], x_ref[2 * i + 1, fs:]], axis=1)
        grad = dot(dgu, jnp.concatenate([x, pad], axis=0))
        part = pl.ds(2 * i * LANES, 2 * LANES)
        gg_ref[:, part] = grad[:fs]
        gu_ref[:, part] = grad[fs:]


def combine_back_body(base_ref, r_ref, p_ref, ids_ref, m_ref):
    h, l = r_ref.shape[0], m_ref.shape[0]
    g = LANES // l
    y = dot(stacked(p_ref), stacked(r_ref), 0, 0)
    ids = ids_ref[...]
    i, j = index((ROWS, ROWS))
    up = onehot(j == HELD + i % NEAR)
    routes = jnp.zeros(ids.shape, F4)
    for e in range(h):
        column = gathered_column(dot(up, r_ref[e]), ROWS)
        at_token = jnp.sum(p_ref[e].astype(F4) * column, axis=0, keepdims=True)
        mine = (base_ref[0] + e * l).astype(F4)
        routes = routes + jnp.where(ids == mine, at_token, 0.0)
    at = lane((8, LANES))
    for i in range(l):
        own = split3(jnp.where(at < g, roll(routes, -i * g), 0.0), g)
        m_ref[i] = jnp.concatenate(
            [y[i * g : (i + 1) * g], own, jnp.zeros((8, LANES), F4)], axis=0
        ).astype(BF)


def finish_body(r_ref, t_ref, g_ref):
    total = r_ref[0].astype(F4)
    for i in range(1, r_ref.shape[0]):
        total = total + r_ref[i].astype(F4)
    rows = t_ref.shape[0]
    t_ref[...] = total[:rows].astype(BF)
    g_ref[...] = join3(total[rows : rows + 8], rows)[:, :rows]


def exchange(x, axis):
    return lax.all_to_all(x, axis, split_axis=0, concat_axis=0, tiled=True)


def shards(tokens, target, expert_ids, route_weights, w_gate, w_up, w_down):
    h, l, n = lax.axis_size("eh"), lax.axis_size("el"), lax.axis_size("fsdp")
    g, k = expert_ids.shape
    fs, d = w_gate.shape[1], w_gate.shape[2]
    df = tokens.shape[1]
    mean_load = k * g // (h * l)
    assert df == LANES and g * l == LANES and k == 8 and l == NEAR
    assert min(g, mean_load + mean_load // 2 + 1) == CAP
    wg, wu, wd = w_gate[0], w_up[0], w_down[0]
    held, slots = CAP * h * l, 8 * h * l
    pairs = h // 2
    base = lax.axis_index("el").astype(jnp.int32).reshape(1)

    (message,) = call(
        first_body, [((l, g + 16, df), BF)],
        base, expert_ids.T, route_weights.T, tokens, smem=(0,), hbm=(1, 2, 3),
        scratch=(
            pltpu.VMEM((k, g), jnp.int32), pltpu.VMEM((k, g), F4), pltpu.VMEM((g, df), BF),
            pltpu.SemaphoreType.DMA((3,)),
        ),
        vmem_mib=60, name="first",
    )
    got = exchange(message, "el")
    wgu, wd = call(
        weights_body, [((2 * fs, d), BF), ((fs, d), BF)], wg, wu, wd, name="weights"
    )
    to_far = ((h, ROWS, df), BF)
    message, place, ids = call(
        dispatch_body, [to_far, to_far, ((8, LANES), F4)],
        base, got, smem=(0,), name="dispatch",
    )
    got = exchange(message, "eh")
    message, scale = call(
        expert_in_body,
        [((n, fs + held, df), BF), ((pairs, 2 * HELD, LANES), F4)],
        got, wd, name="expert_in",
    )
    rows = exchange(message, "fsdp")
    packed = (n, fs * slots // LANES, LANES)
    gate, up, wd_f, message = call(
        hidden_body,
        [((fs, slots), F4), ((fs, slots), F4), ((n * fs, df), BF), (packed, BF)],
        rows, wgu, name="hidden",
    )
    got = exchange(message, "fsdp")
    out, hidden, message = call(
        expert_out_body,
        [((slots, df), F4), ((n * fs, slots), BF), to_far],
        got, wd_f, scale, name="expert_out",
    )
    got = exchange(message, "eh")
    (message,) = call(
        combine_body, [((l, l * g + g, df), BF)], got, place, target, name="combine"
    )
    got = exchange(message, "el")
    layer_out, message = call(
        resid_body, [((g, df), BF), to_far], base, got, place, smem=(0,),
        scratch=(pltpu.VMEM((l * g, df), F4),), name="resid",
    )
    got = exchange(message, "eh")
    message, down = call(
        delta_in_body,
        [(packed, BF), ((n, fs, df), BF)],
        got, scale, out, wd_f, hidden, name="delta_in",
    )
    got = exchange(message, "fsdp")
    message, dgu, dots = call(
        delta_body,
        [((n, fs + held, df), BF), ((2 * fs, slots), BF), ((pairs, 2 * l, LANES), F4)],
        got, gate, up, wgu, down, name="delta",
    )
    got = exchange(message, "fsdp")
    message, grad_down, tick = call(
        back_body, [to_far, ((fs, d), F4), ((2 * l, LANES), F4)], got, dots, name="back"
    )
    got = exchange(message, "eh")
    grad_gate, grad_up = call(
        grads_body, [((fs, d), F4)] * 2, tick, rows, dgu, name="grads"
    )
    (message,) = call(
        combine_back_body, [((l, g + 16, df), BF)],
        base, got, place, ids, smem=(0,), name="combine_back",
    )
    got = exchange(message, "el")
    grad_tokens, grad_route = call(
        finish_body, [((g, df), BF), ((8, g), F4)], got, name="finish"
    )
    return (
        layer_out, grad_tokens, grad_route.T, grad_gate[None], grad_up[None], grad_down[None]
    )


def solution(mesh):
    experts, fsdp = mesh.devices.shape
    split = Mesh(mesh.devices.reshape(experts // NEAR, NEAR, fsdp), ("eh", "el", "fsdp"))
    e = ("eh", "el")
    return jax.shard_map(
        shards,
        mesh=split,
        in_specs=(
            P(e, "fsdp"),
            P(e, "fsdp"),
            P(e, None),
            P(e, None),
            P(e, "fsdp", None),
            P(e, "fsdp", None),
            P(e, "fsdp", None),
        ),
        out_specs=(
            P(e, "fsdp"),
            P(e, "fsdp"),
            P(e, None),
            P(e, "fsdp", None),
            P(e, "fsdp", None),
            P(e, "fsdp", None),
        ),
        check_vma=False,
    )
```

```python
import functools

import jax
import jax.numpy as jnp
from jax import lax
from jax.experimental import pallas as pl
from jax.experimental.pallas import tpu as pltpu
from jax.sharding import Mesh, PartitionSpec as P

BF = jnp.bfloat16
F4 = jnp.float32
LANES = 128
HI = 8
CAP = 7


def dot(a, b, ca=1, cb=0):
    return lax.dot_general(a, b, (((ca,), (cb,)), ((), ())), preferred_element_type=F4)


def call(body, outs, *args, smem=(), hbm=(), scratch=(), vmem_mib=16, name=None):
    specs = [
        pl.BlockSpec(
            memory_space=pltpu.SMEM if i in smem else pltpu.HBM if i in hbm else pltpu.VMEM
        )
        for i in range(len(args))
    ]
    nbytes = sum(a.size * a.dtype.itemsize for a in args)
    shapes = [jax.ShapeDtypeStruct(s, d) for s, d in outs]
    return pl.pallas_call(
        body,
        out_shape=shapes,
        in_specs=specs,
        out_specs=[pl.BlockSpec(memory_space=pltpu.VMEM) for _ in shapes],
        scratch_shapes=list(scratch),
        compiler_params=pltpu.CompilerParams(vmem_limit_bytes=vmem_mib * 1024 * 1024),
        cost_estimate=pl.CostEstimate(
            flops=100_000_000, bytes_accessed=int(nbytes), transcendentals=0
        ),
        name=name,
    )(*args)


def lane(shape):
    return lax.broadcasted_iota(jnp.int32, shape, 1)


def roll(x, by):
    by = by % LANES
    return x if by == 0 else pltpu.roll(x, by, 1)


def split3(x, step):
    hi = x.astype(BF).astype(F4)
    rest = x - hi
    mid = rest.astype(BF).astype(F4)
    return hi + roll(mid, step) + roll(rest - mid, 2 * step)


def join3(x, step):
    return x + roll(x, -step) + roll(x, -2 * step)


def column_tile(column, h):
    at = lane((h, LANES))
    tile = jnp.zeros((h, LANES), F4)
    for c in range(CAP):
        tile = jnp.where(at == c, column[c * h : (c + 1) * h], tile)
    return tile


def scale_rows(rows, tile, h):
    return jnp.concatenate(
        [rows[c * h : (c + 1) * h] * tile[:, c : c + 1] for c in range(CAP)], axis=0
    )


def blocks_to_rows(x):
    return jnp.concatenate(
        [x[:, i * LANES : (i + 1) * LANES] for i in range(x.shape[1] // LANES)], axis=0
    )


def rows_to_blocks(x, rows):
    return jnp.concatenate(
        [x[i * rows : (i + 1) * rows] for i in range(x.shape[0] // rows)], axis=1
    )


def first_body(base_ref, ids_in, weights_in, t_in, m_ref, ids_ref, weights_ref, t_ref, sem):
    k, g = ids_ref.shape
    pairs = ((ids_in, ids_ref), (weights_in, weights_ref), (t_in, t_ref))
    copies = [pltpu.make_async_copy(a, b, sem.at[i]) for i, (a, b) in enumerate(pairs)]
    for copy in copies:
        copy.start()
    for copy in copies:
        copy.wait()
    w = weights_ref[...]
    hi = w.astype(BF)
    rest = w - hi.astype(F4)
    mid = rest.astype(BF)
    low = (rest - mid.astype(F4)).astype(BF)
    row = lax.broadcasted_iota(jnp.int32, (g, LANES), 0)
    col = lane((g, LANES))
    meta = jnp.zeros((k, LANES), F4)
    for i, part in enumerate((ids_ref[...].astype(F4).astype(BF), hi, mid, low)):
        move = jnp.where(col == row + i * g, 1.0, 0.0).astype(BF)
        meta = meta + dot(part, move)
    message = jnp.concatenate([t_ref[...].astype(F4), meta], axis=0).astype(BF)
    for i in range(m_ref.shape[0]):
        m_ref[i] = message


def weights_body(wg_ref, wu_ref, wd_ref, wgu_ref, wd_out_ref):
    fs = wg_ref.shape[0]
    wgu_ref[:fs] = wg_ref[...]
    wgu_ref[fs:] = wu_ref[...]
    wd_out_ref[...] = wd_ref[...]


def dispatch_body(base_ref, r_ref, m_ref, p_ref, ids_ref):
    h, l = r_ref.shape[0], m_ref.shape[0]
    g = 32
    width = h * g
    per = LANES // g
    at = lane((8, LANES))
    metas = [r_ref[i].astype(F4)[g : g + 8] for i in range(h)]

    def gathered(parts, start):
        out = []
        for q in range(h // per):
            acc = jnp.zeros((8, LANES), F4)
            for i in range(per):
                moved = roll(parts[q * per + i], i * g - start)
                acc = jnp.where(at // g == i, moved, acc)
            out.append(acc)
        return jnp.concatenate(out, axis=1)

    ids = gathered(metas, 0)
    weights = gathered([join3(m, g) for m in metas], g)
    ids_ref[...] = ids
    mine = (lax.broadcasted_iota(jnp.int32, (l, width), 0) + base_ref[0]).astype(F4)
    named = jnp.zeros((l, width), F4)
    weight_at = jnp.zeros((l, width), F4)
    for k in range(8):
        hit = ids[k : k + 1] == mine
        named = named + jnp.where(hit, 1.0, 0.0)
        weight_at = weight_at + jnp.where(hit, weights[k : k + 1], 0.0)
    row = lax.broadcasted_iota(jnp.int32, (width, width), 0)
    col = lane((width, width))
    before = jnp.where((row // g == col // g) & (row < col), 1.0, 0.0).astype(BF)
    rank = dot(named.astype(BF), before)
    rank = jnp.where(named > 0.0, rank, -1.0)
    block = lane((h, width)) // g == lax.broadcasted_iota(jnp.int32, (h, width), 0)
    x = jnp.concatenate([r_ref[i][:g] for i in range(h)], axis=0)
    for e in range(l):
        own = jnp.broadcast_to(rank[e : e + 1], (h, width))
        place = jnp.concatenate(
            [jnp.where(block & (own == float(c)), 1.0, 0.0) for c in range(8)], axis=0
        )
        column = jnp.sum(place * weight_at[e : e + 1], axis=1, keepdims=True)
        place = place.astype(BF)
        p_ref[e] = place
        rows = dot(place, x)
        tile = split3(column_tile(column, h), 8)
        m_ref[e] = jnp.concatenate([rows[: CAP * h], tile], axis=0).astype(BF)


def expert_in_body(r_ref, wd_ref, f_ref, w_ref):
    l, h = r_ref.shape[0], r_ref.shape[1] // 8
    fs = wd_ref.shape[0]
    rows = []
    for e in range(l):
        v = r_ref[e].astype(F4)
        rows.append(v[: CAP * h])
        w_ref[e] = join3(v[CAP * h :], 8)
    x = jnp.concatenate(rows, axis=0).astype(BF)
    for d in range(f_ref.shape[0]):
        f_ref[d, :fs] = wd_ref[:, d * LANES : (d + 1) * LANES]
        f_ref[d, fs:] = x


def hidden_body(r_ref, wgu_ref, gate_ref, up_ref, wd_ref, f_ref):
    n, fs = r_ref.shape[0], gate_ref.shape[0]
    slots = gate_ref.shape[1]
    held = r_ref.shape[1] - fs
    pad = jnp.zeros((slots - held, 2 * LANES), BF)
    total = jnp.zeros((2 * fs, slots), F4)
    for i in range(n // 2):
        x = jnp.concatenate([r_ref[2 * i, fs:], r_ref[2 * i + 1, fs:]], axis=1)
        x = jnp.concatenate([x, pad], axis=0)
        w = wgu_ref[:, 2 * i * LANES : 2 * (i + 1) * LANES]
        total = total + dot(w, x, 1, 1)
    gate, up = total[:fs], total[fs:]
    gate_ref[...] = gate
    up_ref[...] = up
    hidden = gate * jax.nn.sigmoid(gate) * up
    last = hidden[:, 3 * LANES :]
    last = last[: fs // 2] + roll(last[fs // 2 :], LANES // 2)
    message = blocks_to_rows(hidden[:, : 3 * LANES])
    message = jnp.concatenate([message, last], axis=0).astype(BF)
    for d in range(n):
        f_ref[d] = message
        wd_ref[d * fs : (d + 1) * fs] = r_ref[d, :fs]


def expert_out_body(r_ref, wd_ref, w_ref, out_ref, h_ref, m_ref):
    n, l, h = r_ref.shape[0], w_ref.shape[0], w_ref.shape[1]
    fs = wd_ref.shape[0] // n
    parts = []
    for i in range(n):
        v = r_ref[i].astype(F4)
        last = v[3 * fs :]
        left = lane(last.shape) < LANES // 2
        halves = [jnp.where(left, x, 0.0) for x in (last, roll(last, LANES // 2))]
        v = jnp.concatenate([v[: 3 * fs]] + halves, axis=0)
        parts.append(rows_to_blocks(v, fs).astype(BF))
    hidden = jnp.concatenate(parts, axis=0)
    h_ref[...] = hidden
    out = dot(hidden, wd_ref[...], 0, 0)
    out_ref[...] = out
    for e in range(l):
        rows = out[e * CAP * h : (e + 1) * CAP * h]
        rows = scale_rows(rows, w_ref[e], h)
        m_ref[e] = jnp.concatenate([rows, jnp.zeros((h, LANES), F4)], axis=0).astype(BF)


def combine_body(r_ref, p_ref, m_ref):
    l, rows = r_ref.shape[0], r_ref.shape[1]
    x = jnp.concatenate([r_ref[i] for i in range(l)], axis=0)
    p = jnp.concatenate([p_ref[i] for i in range(l)], axis=0)
    y = dot(p, x, 0, 0).astype(BF)
    g = m_ref.shape[1]
    for i in range(m_ref.shape[0]):
        m_ref[i] = y[i * g : (i + 1) * g]


def resid_body(r_ref, t_ref, o_ref, m_ref):
    total = r_ref[0].astype(F4)
    for i in range(1, r_ref.shape[0]):
        total = total + r_ref[i].astype(F4)
    layer = total.astype(BF)
    o_ref[...] = layer
    resid = (layer.astype(F4) - t_ref[...].astype(F4)).astype(BF)
    for i in range(m_ref.shape[0]):
        m_ref[i] = resid


def redispatch_body(r_ref, p_ref, m_ref):
    x = jnp.concatenate([r_ref[i] for i in range(r_ref.shape[0])], axis=0)
    for e in range(p_ref.shape[0]):
        m_ref[e] = dot(p_ref[e], x).astype(BF)


def delta_in_body(r_ref, w_ref, out_ref, wd_ref, h_ref, f_ref, g_ref):
    l, h = w_ref.shape[0], w_ref.shape[1]
    n, fs = f_ref.shape[0], f_ref.shape[1] // 4
    slots = h_ref.shape[1]
    rows, tiles = [], []
    for e in range(l):
        resid = r_ref[e].astype(F4)[: CAP * h]
        out = out_ref[e * CAP * h : (e + 1) * CAP * h]
        column = jnp.sum(resid * out, axis=1, keepdims=True)
        tiles.append(split3(column_tile(column, h), 8))
        rows.append(scale_rows(resid, w_ref[e], h))
    rows.append(jnp.zeros((slots - l * CAP * h, LANES), F4))
    scaled = jnp.concatenate(rows, axis=0).astype(BF)
    half = l // 2
    packed = roll(jnp.concatenate(tiles[:half], axis=0), 64) + roll(
        jnp.concatenate(tiles[half:], axis=0), 88
    )
    packed = jnp.concatenate([packed, jnp.zeros((fs - packed.shape[0], LANES), F4)], axis=0)
    for d in range(n):
        part = dot(wd_ref[d * fs : (d + 1) * fs], scaled, 1, 1)
        message = blocks_to_rows(part)
        last = message[3 * fs :] + packed
        f_ref[d] = jnp.concatenate([message[: 3 * fs], last], axis=0).astype(BF)
        g_ref[d] = dot(h_ref[d * fs : (d + 1) * fs], scaled).astype(BF)


def delta_body(r_ref, gate_ref, up_ref, wgu_ref, gd_ref, f_ref, dgu_ref, dot_ref):
    n, fs = f_ref.shape[0], gate_ref.shape[0]
    l, h = dot_ref.shape[0], dot_ref.shape[1]
    total = r_ref[0].astype(F4)
    for i in range(1, n):
        total = total + r_ref[i].astype(F4)
    packed = total[3 * fs : 3 * fs + l * h // 2]
    first, second = join3(roll(packed, -64), 8), join3(roll(packed, -88), 8)
    at = lane((h, LANES))
    for e in range(l):
        source = first if e < l // 2 else second
        i = e % (l // 2)
        dot_ref[e] = jnp.where(at < CAP, source[i * h : (i + 1) * h], 0.0)
    dh = rows_to_blocks(total, fs)
    gate, up = gate_ref[...], up_ref[...]
    s = jax.nn.sigmoid(gate)
    dgate = (dh * up * s * (1.0 + gate * (1.0 - s))).astype(BF)
    dup = (dh * gate * s).astype(BF)
    dgu = jnp.concatenate([dgate, dup], axis=0)
    dgu_ref[...] = dgu
    held = CAP * h * l
    for i in range(n // 2):
        back = dot(dgu, wgu_ref[:, 2 * i * LANES : 2 * (i + 1) * LANES], 0, 0)
        back = back[:held].astype(BF)
        for d in (2 * i, 2 * i + 1):
            own = (d - 2 * i) * LANES
            f_ref[d, :fs] = gd_ref[d]
            f_ref[d, fs:] = back[:, own : own + LANES]


def back_body(r_ref, dot_ref, m_ref, gd_ref):
    l, h = dot_ref.shape[0], dot_ref.shape[1]
    fs = r_ref.shape[1] - CAP * h * l
    total = r_ref[0, fs:].astype(F4)
    for i in range(1, r_ref.shape[0]):
        total = total + r_ref[i, fs:].astype(F4)
    for e in range(l):
        rows = total[e * CAP * h : (e + 1) * CAP * h]
        m_ref[e] = jnp.concatenate([rows, split3(dot_ref[e], 8)], axis=0).astype(BF)
    for i in range(r_ref.shape[0]):
        gd_ref[:, i * LANES : (i + 1) * LANES] = r_ref[i, :fs].astype(F4)


def grads_body(tick_ref, x_ref, dgu_ref, gg_ref, gu_ref):
    n, fs = x_ref.shape[0], gg_ref.shape[0]
    dgu = dgu_ref[...]
    pad = jnp.zeros((dgu.shape[1] - x_ref.shape[1] + fs, 2 * LANES), BF)
    for i in range(n // 2):
        x = jnp.concatenate([x_ref[2 * i, fs:], x_ref[2 * i + 1, fs:]], axis=1)
        grad = dot(dgu, jnp.concatenate([x, pad], axis=0))
        part = pl.ds(2 * i * LANES, 2 * LANES)
        gg_ref[:, part] = grad[:fs]
        gu_ref[:, part] = grad[fs:]


def combine_back_body(base_ref, r_ref, p_ref, ids_ref, m_ref, tick_ref):
    l, hosts = r_ref.shape[0], m_ref.shape[0]
    h = hosts
    g = 32
    per = LANES // g
    x = jnp.concatenate([r_ref[i] for i in range(l)], axis=0)
    p = jnp.concatenate([p_ref[i] for i in range(l)], axis=0)
    y = dot(p, x, 0, 0)
    ids = ids_ref[...]
    tick_ref[...] = ids[:, :LANES]
    routes = jnp.zeros(ids.shape, F4)
    for e in range(l):
        tile = join3(r_ref[e].astype(F4)[CAP * h :], 8)
        place = p_ref[e].astype(F4)
        acc = jnp.zeros((h, ids.shape[1]), F4)
        for c in range(CAP):
            acc = acc + place[c * h : (c + 1) * h] * tile[:, c : c + 1]
        at_token = jnp.sum(acc, axis=0, keepdims=True)
        mine = (base_ref[0] + e).astype(F4)
        routes = routes + jnp.where(ids == mine, at_token, 0.0)
    at = lane((8, LANES))
    for i in range(hosts):
        q = i // per
        own = roll(routes[:, q * LANES : (q + 1) * LANES], -(i % per) * g)
        own = split3(jnp.where(at < g, own, 0.0), g)
        m_ref[i] = jnp.concatenate([y[i * g : (i + 1) * g], own], axis=0).astype(BF)


def finish_body(r_ref, t_ref, g_ref):
    total = r_ref[0].astype(F4)
    for i in range(1, r_ref.shape[0]):
        total = total + r_ref[i].astype(F4)
    rows = t_ref.shape[0]
    t_ref[...] = total[:rows].astype(BF)
    g_ref[...] = join3(total[rows : rows + 8], rows)[:, :rows]


def exchange(x, axis):
    return lax.all_to_all(x, axis, split_axis=0, concat_axis=0, tiled=True)


def shards(tokens, target, expert_ids, route_weights, w_gate, w_up, w_down):
    h, l, n = lax.axis_size("eh"), lax.axis_size("el"), lax.axis_size("fsdp")
    g, k = expert_ids.shape
    fs, d = w_gate.shape[1], w_gate.shape[2]
    df = tokens.shape[1]
    mean_load = k * g // (h * l)
    assert df == LANES and g == 32 and k == 8 and h % 8 == 0
    assert min(g, mean_load + mean_load // 2 + 1) == CAP
    wg, wu, wd = w_gate[0], w_up[0], w_down[0]
    held, slots = CAP * h * l, 8 * h * l
    base = (lax.axis_index("eh") * l).astype(jnp.int32).reshape(1)

    (message,) = call(
        first_body, [((h, g + 8, df), BF)],
        base, expert_ids.T, route_weights.T, tokens, smem=(0,), hbm=(1, 2, 3),
        scratch=(
            pltpu.VMEM((k, g), jnp.int32), pltpu.VMEM((k, g), F4), pltpu.VMEM((g, df), BF),
            pltpu.SemaphoreType.DMA((3,)),
        ),
        vmem_mib=60, name="first",
    )
    got = exchange(message, "eh")
    wgu, wd = call(
        weights_body, [((2 * fs, d), BF), ((fs, d), BF)], wg, wu, wd, name="weights"
    )
    message, place, ids = call(
        dispatch_body,
        [((l, 8 * h, df), BF), ((l, 8 * h, h * g), BF), ((8, h * g), F4)],
        base, got, smem=(0,), name="dispatch",
    )
    got = exchange(message, "el")
    message, w_tile = call(
        expert_in_body,
        [((n, fs + held, df), BF), ((l, h, LANES), F4)],
        got, wd, name="expert_in",
    )
    rows = exchange(message, "fsdp")
    packed = (n, fs * slots // LANES, LANES)
    half_packed = (n, fs * slots // LANES - fs // 2, LANES)
    gate, up, wd_f, message = call(
        hidden_body,
        [((fs, slots), F4), ((fs, slots), F4), ((n * fs, df), BF), (half_packed, BF)],
        rows, wgu, name="hidden",
    )
    got = exchange(message, "fsdp")
    out, hidden, message = call(
        expert_out_body,
        [((slots, df), F4), ((n * fs, slots), BF), ((l, 8 * h, df), BF)],
        got, wd_f, w_tile, name="expert_out",
    )
    got = exchange(message, "el")
    (message,) = call(combine_body, [((h, g, df), BF)], got, place, name="combine")
    got = exchange(message, "eh")
    layer_out, message = call(
        resid_body, [((g, df), BF), ((h, g, df), BF)], got, target, name="resid"
    )
    got = exchange(message, "eh")
    (message,) = call(
        redispatch_body, [((l, 8 * h, df), BF)], got, place, name="redispatch"
    )
    got = exchange(message, "el")
    message, down = call(
        delta_in_body,
        [(packed, BF), ((n, fs, df), BF)],
        got, w_tile, out, wd_f, hidden, name="delta_in",
    )
    got = exchange(message, "fsdp")
    message, dgu, dots = call(
        delta_body,
        [((n, fs + held, df), BF), ((2 * fs, slots), BF), ((l, h, LANES), F4)],
        got, gate, up, wgu, down, name="delta",
    )
    got = exchange(message, "fsdp")
    message, grad_down = call(
        back_body, [((l, 8 * h, df), BF), ((fs, d), F4)], got, dots, name="back"
    )
    got = exchange(message, "el")
    message, tick = call(
        combine_back_body,
        [((h, g + 8, df), BF), ((8, LANES), F4)],
        base, got, place, ids, smem=(0,), name="combine_back",
    )
    got = exchange(message, "eh")
    grad_gate, grad_up = call(
        grads_body, [((fs, d), F4)] * 2, tick, rows, dgu, name="grads"
    )
    grad_tokens, grad_route = call(
        finish_body, [((g, df), BF), ((8, g), F4)], got, name="finish"
    )
    return (
        layer_out, grad_tokens, grad_route.T, grad_gate[None], grad_up[None], grad_down[None]
    )


def solution(mesh):
    experts, fsdp = mesh.devices.shape
    split = Mesh(mesh.devices.reshape(HI, experts // HI, fsdp), ("eh", "el", "fsdp"))
    e = ("eh", "el")
    return jax.shard_map(
        shards,
        mesh=split,
        in_specs=(
            P(e, "fsdp"),
            P(e, "fsdp"),
            P(e, None),
            P(e, None),
            P(e, "fsdp", None),
            P(e, "fsdp", None),
            P(e, "fsdp", None),
        ),
        out_specs=(
            P(e, "fsdp"),
            P(e, "fsdp"),
            P(e, None),
            P(e, "fsdp", None),
            P(e, "fsdp", None),
            P(e, "fsdp", None),
        ),
        check_vma=False,
    )
```

```python
import functools

import jax
import jax.numpy as jnp
from jax import lax
from jax.experimental import pallas as pl
from jax.experimental.pallas import tpu as pltpu
from jax.sharding import Mesh, PartitionSpec as P

BF = jnp.bfloat16
F4 = jnp.float32
LANES = 128
HI = 8
CAP = 7


def dot(a, b, ca=1, cb=0):
    return lax.dot_general(a, b, (((ca,), (cb,)), ((), ())), preferred_element_type=F4)


def call(body, outs, *args, smem=(), hbm=(), scratch=(), vmem_mib=16, name=None):
    specs = [
        pl.BlockSpec(
            memory_space=pltpu.SMEM if i in smem else pltpu.HBM if i in hbm else pltpu.VMEM
        )
        for i in range(len(args))
    ]
    nbytes = sum(a.size * a.dtype.itemsize for a in args)
    shapes = [jax.ShapeDtypeStruct(s, d) for s, d in outs]
    return pl.pallas_call(
        body,
        out_shape=shapes,
        in_specs=specs,
        out_specs=[pl.BlockSpec(memory_space=pltpu.VMEM) for _ in shapes],
        scratch_shapes=list(scratch),
        compiler_params=pltpu.CompilerParams(vmem_limit_bytes=vmem_mib * 1024 * 1024),
        cost_estimate=pl.CostEstimate(
            flops=100_000_000, bytes_accessed=int(nbytes), transcendentals=0
        ),
        name=name,
    )(*args)


def lane(shape):
    return lax.broadcasted_iota(jnp.int32, shape, 1)


def roll(x, by):
    by = by % LANES
    return x if by == 0 else pltpu.roll(x, by, 1)


def split3(x, step):
    hi = x.astype(BF).astype(F4)
    rest = x - hi
    mid = rest.astype(BF).astype(F4)
    return hi + roll(mid, step) + roll(rest - mid, 2 * step)


def join3(x, step):
    return x + roll(x, -step) + roll(x, -2 * step)


def column_tile(column, h):
    at = lane((h, LANES))
    tile = jnp.zeros((h, LANES), F4)
    for c in range(CAP):
        tile = jnp.where(at == c, column[c * h : (c + 1) * h], tile)
    return tile


def scale_rows(rows, tile, h):
    return jnp.concatenate(
        [rows[c * h : (c + 1) * h] * tile[:, c : c + 1] for c in range(CAP)], axis=0
    )


def blocks_to_rows(x):
    return jnp.concatenate(
        [x[:, i * LANES : (i + 1) * LANES] for i in range(x.shape[1] // LANES)], axis=0
    )


def rows_to_blocks(x, rows):
    return jnp.concatenate(
        [x[i * rows : (i + 1) * rows] for i in range(x.shape[0] // rows)], axis=1
    )


def first_body(base_ref, ids_in, weights_in, t_in, m_ref, ids_ref, weights_ref, t_ref, sem):
    k, g = ids_ref.shape
    pairs = ((ids_in, ids_ref), (weights_in, weights_ref), (t_in, t_ref))
    copies = [pltpu.make_async_copy(a, b, sem.at[i]) for i, (a, b) in enumerate(pairs)]
    for copy in copies:
        copy.start()
    for copy in copies:
        copy.wait()
    w = weights_ref[...]
    hi = w.astype(BF)
    rest = w - hi.astype(F4)
    mid = rest.astype(BF)
    low = (rest - mid.astype(F4)).astype(BF)
    row = lax.broadcasted_iota(jnp.int32, (g, LANES), 0)
    col = lane((g, LANES))
    meta = jnp.zeros((k, LANES), F4)
    for i, part in enumerate((ids_ref[...].astype(F4).astype(BF), hi, mid, low)):
        move = jnp.where(col == row + i * g, 1.0, 0.0).astype(BF)
        meta = meta + dot(part, move)
    message = jnp.concatenate([t_ref[...].astype(F4), meta], axis=0).astype(BF)
    for i in range(m_ref.shape[0]):
        m_ref[i] = message


def weights_body(wg_ref, wu_ref, wd_ref, wgu_ref, wd_out_ref):
    fs = wg_ref.shape[0]
    wgu_ref[:fs] = wg_ref[...]
    wgu_ref[fs:] = wu_ref[...]
    wd_out_ref[...] = wd_ref[...]


def dispatch_body(base_ref, r_ref, m_ref):
    h, l = r_ref.shape[0], m_ref.shape[0]
    g = 32
    width = h * g
    per = LANES // g
    at = lane((8, LANES))
    metas = [r_ref[i].astype(F4)[g : g + 8] for i in range(h)]

    def gathered(parts, start):
        out = []
        for q in range(h // per):
            acc = jnp.zeros((8, LANES), F4)
            for i in range(per):
                moved = roll(parts[q * per + i], i * g - start)
                acc = jnp.where(at // g == i, moved, acc)
            out.append(acc)
        return jnp.concatenate(out, axis=1)

    ids = gathered(metas, 0)
    weights = gathered([join3(m, g) for m in metas], g)
    mine = (lax.broadcasted_iota(jnp.int32, (l, width), 0) * h + base_ref[0]).astype(F4)
    named = jnp.zeros((l, width), F4)
    weight_at = jnp.zeros((l, width), F4)
    for k in range(8):
        hit = ids[k : k + 1] == mine
        named = named + jnp.where(hit, 1.0, 0.0)
        weight_at = weight_at + jnp.where(hit, weights[k : k + 1], 0.0)
    row = lax.broadcasted_iota(jnp.int32, (width, width), 0)
    col = lane((width, width))
    before = jnp.where((row // g == col // g) & (row < col), 1.0, 0.0).astype(BF)
    rank = dot(named.astype(BF), before)
    rank = jnp.where(named > 0.0, rank, -1.0)
    block = lane((h, width)) // g == lax.broadcasted_iota(jnp.int32, (h, width), 0)
    x = jnp.concatenate([r_ref[i][:g] for i in range(h)], axis=0)
    number = (lane((1, width)) % g + 1).astype(F4)
    for e in range(l):
        own = jnp.broadcast_to(rank[e : e + 1], (h, width))
        place = jnp.concatenate(
            [jnp.where(block & (own == float(c)), 1.0, 0.0) for c in range(8)], axis=0
        )
        column = jnp.sum(place * weight_at[e : e + 1], axis=1, keepdims=True)
        token = jnp.sum(place * number, axis=1, keepdims=True)
        rows = dot(place.astype(BF), x)
        tile = split3(column_tile(column, h), 8) + roll(column_tile(token, h), 24)
        m_ref[e] = jnp.concatenate([rows[: CAP * h], tile], axis=0).astype(BF)


def expert_in_body(r_ref, wd_ref, f_ref, w_ref, k_ref):
    h, l = r_ref.shape[0], w_ref.shape[0]
    fs = wd_ref.shape[0]
    run = CAP * l
    rows, tiles = [], []
    for e in range(h):
        v = r_ref[e].astype(F4)
        rows.append(v[:run])
        tiles.append(v[run:])
    i = lax.broadcasted_iota(jnp.int32, (h * run, LANES), 0)
    source = (i % h * run + i % run // h * l + i // run)[:, :1]
    move = jnp.where(lane((h * run, h * run)) == source, 1.0, 0.0).astype(BF)
    x = dot(move, jnp.concatenate(rows, axis=0).astype(BF)).astype(BF)
    i = lax.broadcasted_iota(jnp.int32, (h * l, h * l), 0)
    move = jnp.where(lane((h * l, h * l)) == i % h * l + i // h, 1.0, 0.0).astype(BF)
    meta = dot(move, jnp.concatenate(tiles, axis=0).astype(BF))
    weights = join3(meta, 8)
    tokens = jnp.where(lane(meta.shape) < CAP, roll(meta, -24), 0.0)
    for e in range(l):
        w_ref[e] = weights[e * h : (e + 1) * h]
        k_ref[e] = tokens[e * h : (e + 1) * h]
    for d in range(f_ref.shape[0]):
        f_ref[d, :fs] = wd_ref[:, d * LANES : (d + 1) * LANES]
        f_ref[d, fs:] = x


def hidden_body(r_ref, wgu_ref, gate_ref, up_ref, wd_ref, f_ref):
    n, fs = r_ref.shape[0], gate_ref.shape[0]
    slots = gate_ref.shape[1]
    held = r_ref.shape[1] - fs
    pad = jnp.zeros((slots - held, 2 * LANES), BF)
    total = jnp.zeros((2 * fs, slots), F4)
    for i in range(n // 2):
        x = jnp.concatenate([r_ref[2 * i, fs:], r_ref[2 * i + 1, fs:]], axis=1)
        x = jnp.concatenate([x, pad], axis=0)
        w = wgu_ref[:, 2 * i * LANES : 2 * (i + 1) * LANES]
        total = total + dot(w, x, 1, 1)
    gate, up = total[:fs], total[fs:]
    gate_ref[...] = gate
    up_ref[...] = up
    hidden = gate * jax.nn.sigmoid(gate) * up
    last = hidden[:, 3 * LANES :]
    last = last[: fs // 2] + roll(last[fs // 2 :], LANES // 2)
    message = blocks_to_rows(hidden[:, : 3 * LANES])
    message = jnp.concatenate([message, last], axis=0).astype(BF)
    for d in range(n):
        f_ref[d] = message
        wd_ref[d * fs : (d + 1) * fs] = r_ref[d, :fs]


def expert_out_body(r_ref, wd_ref, w_ref, k_ref, out_ref, h_ref, m_ref):
    n, l, h = r_ref.shape[0], w_ref.shape[0], w_ref.shape[1]
    fs = wd_ref.shape[0] // n
    parts = []
    for i in range(n):
        v = r_ref[i].astype(F4)
        last = v[3 * fs :]
        left = lane(last.shape) < LANES // 2
        halves = [jnp.where(left, x, 0.0) for x in (last, roll(last, LANES // 2))]
        v = jnp.concatenate([v[: 3 * fs]] + halves, axis=0)
        parts.append(rows_to_blocks(v, fs).astype(BF))
    hidden = jnp.concatenate(parts, axis=0)
    h_ref[...] = hidden
    out = dot(hidden, wd_ref[...], 0, 0)
    out_ref[...] = out
    for e in range(l):
        rows = out[e * CAP * h : (e + 1) * CAP * h]
        rows = scale_rows(rows, w_ref[e], h)
        m_ref[e] = jnp.concatenate([rows, k_ref[e]], axis=0).astype(BF)


def combine_body(r_ref, m_ref, p_ref):
    l, h, g = r_ref.shape[0], m_ref.shape[0], m_ref.shape[1]
    shape = (h, h * g)
    block = lane(shape) // g == lax.broadcasted_iota(jnp.int32, shape, 0)
    number = jnp.where(block, lane(shape) % g + 1, 0).astype(F4)
    number = jnp.where(block, number, -1.0)
    places = []
    for e in range(l):
        tile = r_ref[e].astype(F4)[CAP * h :]
        place = [jnp.where(number == tile[:, c : c + 1], 1.0, 0.0) for c in range(CAP)]
        place = jnp.concatenate(place + [jnp.zeros(shape, F4)], axis=0).astype(BF)
        p_ref[e] = place
        places.append(place)
    x = jnp.concatenate([r_ref[i] for i in range(l)], axis=0)
    y = dot(jnp.concatenate(places, axis=0), x, 0, 0).astype(BF)
    for i in range(h):
        m_ref[i] = y[i * g : (i + 1) * g]


def resid_body(r_ref, t_ref, o_ref, m_ref):
    total = r_ref[0].astype(F4)
    for i in range(1, r_ref.shape[0]):
        total = total + r_ref[i].astype(F4)
    layer = total.astype(BF)
    o_ref[...] = layer
    resid = (layer.astype(F4) - t_ref[...].astype(F4)).astype(BF)
    for i in range(m_ref.shape[0]):
        m_ref[i] = resid


def redispatch_body(r_ref, p_ref, m_ref):
    x = jnp.concatenate([r_ref[i] for i in range(r_ref.shape[0])], axis=0)
    for e in range(p_ref.shape[0]):
        m_ref[e] = dot(p_ref[e], x).astype(BF)


def delta_in_body(r_ref, w_ref, out_ref, wd_ref, h_ref, f_ref, g_ref):
    l, h = w_ref.shape[0], w_ref.shape[1]
    n, fs = f_ref.shape[0], f_ref.shape[1] // 4
    slots = h_ref.shape[1]
    rows, tiles = [], []
    for e in range(l):
        resid = r_ref[e].astype(F4)[: CAP * h]
        out = out_ref[e * CAP * h : (e + 1) * CAP * h]
        column = jnp.sum(resid * out, axis=1, keepdims=True)
        tiles.append(split3(column_tile(column, h), 8))
        rows.append(scale_rows(resid, w_ref[e], h))
    rows.append(jnp.zeros((slots - l * CAP * h, LANES), F4))
    scaled = jnp.concatenate(rows, axis=0).astype(BF)
    half = l // 2
    packed = roll(jnp.concatenate(tiles[:half], axis=0), 64) + roll(
        jnp.concatenate(tiles[half:], axis=0), 88
    )
    packed = jnp.concatenate([packed, jnp.zeros((fs - packed.shape[0], LANES), F4)], axis=0)
    for d in range(n):
        part = dot(wd_ref[d * fs : (d + 1) * fs], scaled, 1, 1)
        message = blocks_to_rows(part)
        last = message[3 * fs :] + packed
        f_ref[d] = jnp.concatenate([message[: 3 * fs], last], axis=0).astype(BF)
        g_ref[d] = dot(h_ref[d * fs : (d + 1) * fs], scaled).astype(BF)


def delta_body(r_ref, gate_ref, up_ref, wgu_ref, gd_ref, f_ref, dgu_ref, dot_ref):
    n, fs = f_ref.shape[0], gate_ref.shape[0]
    l, h = dot_ref.shape[0], dot_ref.shape[1]
    total = r_ref[0].astype(F4)
    for i in range(1, n):
        total = total + r_ref[i].astype(F4)
    packed = total[3 * fs : 3 * fs + l * h // 2]
    first, second = join3(roll(packed, -64), 8), join3(roll(packed, -88), 8)
    at = lane((h, LANES))
    for e in range(l):
        source = first if e < l // 2 else second
        i = e % (l // 2)
        dot_ref[e] = jnp.where(at < CAP, source[i * h : (i + 1) * h], 0.0)
    dh = rows_to_blocks(total, fs)
    gate, up = gate_ref[...], up_ref[...]
    s = jax.nn.sigmoid(gate)
    dgate = (dh * up * s * (1.0 + gate * (1.0 - s))).astype(BF)
    dup = (dh * gate * s).astype(BF)
    dgu = jnp.concatenate([dgate, dup], axis=0)
    dgu_ref[...] = dgu
    held = CAP * h * l
    for i in range(n // 2):
        back = dot(dgu, wgu_ref[:, 2 * i * LANES : 2 * (i + 1) * LANES], 0, 0)
        back = back[:held].astype(BF)
        for d in (2 * i, 2 * i + 1):
            own = (d - 2 * i) * LANES
            f_ref[d, :fs] = gd_ref[d]
            f_ref[d, fs:] = back[:, own : own + LANES]


def back_body(r_ref, dot_ref, m_ref, gd_ref):
    l, h = dot_ref.shape[0], dot_ref.shape[1]
    fs = r_ref.shape[1] - CAP * h * l
    total = r_ref[0, fs:].astype(F4)
    for i in range(1, r_ref.shape[0]):
        total = total + r_ref[i, fs:].astype(F4)
    for e in range(l):
        rows = total[e * CAP * h : (e + 1) * CAP * h]
        m_ref[e] = jnp.concatenate([rows, split3(dot_ref[e], 8)], axis=0).astype(BF)
    for i in range(r_ref.shape[0]):
        gd_ref[:, i * LANES : (i + 1) * LANES] = r_ref[i, :fs].astype(F4)


def grads_body(tick_ref, x_ref, dgu_ref, gg_ref, gu_ref):
    n, fs = x_ref.shape[0], gg_ref.shape[0]
    dgu = dgu_ref[...]
    pad = jnp.zeros((dgu.shape[1] - x_ref.shape[1] + fs, 2 * LANES), BF)
    for i in range(n // 2):
        x = jnp.concatenate([x_ref[2 * i, fs:], x_ref[2 * i + 1, fs:]], axis=1)
        grad = dot(dgu, jnp.concatenate([x, pad], axis=0))
        part = pl.ds(2 * i * LANES, 2 * LANES)
        gg_ref[:, part] = grad[:fs]
        gu_ref[:, part] = grad[fs:]


def combine_back_body(r_ref, p_ref, m_ref, tick_ref):
    l, h = r_ref.shape[0], m_ref.shape[0]
    g = p_ref.shape[2] // h
    per = LANES // g
    x = jnp.concatenate([r_ref[i] for i in range(l)], axis=0)
    p = jnp.concatenate([p_ref[i] for i in range(l)], axis=0)
    y = dot(p, x, 0, 0)
    shape = (l, h * g)
    routes = jnp.zeros(shape, F4)
    row = lax.broadcasted_iota(jnp.int32, shape, 0)
    for e in range(l):
        tile = join3(r_ref[e].astype(F4)[CAP * h :], 8)
        place = p_ref[e].astype(F4)
        acc = jnp.zeros((h, h * g), F4)
        for c in range(CAP):
            acc = acc + place[c * h : (c + 1) * h] * tile[:, c : c + 1]
        routes = jnp.where(row == e, jnp.sum(acc, axis=0, keepdims=True), routes)
    tick_ref[...] = routes[:, :LANES]
    at = lane((l, LANES))
    for i in range(h):
        q = i // per
        own = roll(routes[:, q * LANES : (q + 1) * LANES], -(i % per) * g)
        own = split3(jnp.where(at < g, own, 0.0), g)
        m_ref[i] = jnp.concatenate([y[i * g : (i + 1) * g], own], axis=0).astype(BF)


def finish_body(r_ref, ids_ref, t_ref, g_ref):
    h, rows = r_ref.shape[0], t_ref.shape[0]
    l = r_ref.shape[1] - rows
    ids = ids_ref[...]
    total = jnp.zeros((rows, LANES), F4)
    routes = jnp.zeros(ids.shape, F4)
    for i in range(h):
        v = r_ref[i].astype(F4)
        total = total + v[:rows]
        tile = join3(v[rows:], rows)[:, :rows]
        for e in range(l):
            routes = routes + jnp.where(ids == i * l + e, tile[e : e + 1], 0.0)
    t_ref[...] = total.astype(BF)
    g_ref[...] = routes


def exchange(x, axis):
    return lax.all_to_all(x, axis, split_axis=0, concat_axis=0, tiled=True)


def shards(tokens, target, expert_ids, route_weights, w_gate, w_up, w_down):
    h, l, n = lax.axis_size("eh"), lax.axis_size("el"), lax.axis_size("fsdp")
    g, k = expert_ids.shape
    fs, d = w_gate.shape[1], w_gate.shape[2]
    df = tokens.shape[1]
    mean_load = k * g // (h * l)
    assert df == LANES and g == 32 and k == 8 and h == 8 and l == 8
    assert min(g, mean_load + mean_load // 2 + 1) == CAP
    wg, wu, wd = w_gate[0], w_up[0], w_down[0]
    held, slots = CAP * h * l, 8 * h * l
    base = lax.axis_index("el").astype(jnp.int32).reshape(1)

    (message,) = call(
        first_body, [((l, g + 8, df), BF)],
        base, expert_ids.T, route_weights.T, tokens, smem=(0,), hbm=(1, 2, 3),
        scratch=(
            pltpu.VMEM((k, g), jnp.int32), pltpu.VMEM((k, g), F4), pltpu.VMEM((g, df), BF),
            pltpu.SemaphoreType.DMA((3,)),
        ),
        vmem_mib=60, name="first",
    )
    got = exchange(message, "el")
    wgu, wd = call(
        weights_body, [((2 * fs, d), BF), ((fs, d), BF)], wg, wu, wd, name="weights"
    )
    (message,) = call(
        dispatch_body, [((h, 8 * l, df), BF)], base, got, smem=(0,), name="dispatch"
    )
    got = exchange(message, "eh")
    message, w_tile, token_tile = call(
        expert_in_body,
        [((n, fs + held, df), BF), ((l, h, LANES), F4), ((l, h, LANES), F4)],
        got, wd, name="expert_in",
    )
    rows = exchange(message, "fsdp")
    packed = (n, fs * slots // LANES, LANES)
    half_packed = (n, fs * slots // LANES - fs // 2, LANES)
    gate, up, wd_f, message = call(
        hidden_body,
        [((fs, slots), F4), ((fs, slots), F4), ((n * fs, df), BF), (half_packed, BF)],
        rows, wgu, name="hidden",
    )
    got = exchange(message, "fsdp")
    out, hidden, message = call(
        expert_out_body,
        [((slots, df), F4), ((n * fs, slots), BF), ((l, 8 * h, df), BF)],
        got, wd_f, w_tile, token_tile, name="expert_out",
    )
    got = exchange(message, "el")
    message, place = call(
        combine_body, [((h, g, df), BF), ((l, 8 * h, h * g), BF)], got, name="combine"
    )
    got = exchange(message, "eh")
    layer_out, message = call(
        resid_body, [((g, df), BF), ((h, g, df), BF)], got, target, name="resid"
    )
    got = exchange(message, "eh")
    (message,) = call(
        redispatch_body, [((l, 8 * h, df), BF)], got, place, name="redispatch"
    )
    got = exchange(message, "el")
    message, down = call(
        delta_in_body,
        [(packed, BF), ((n, fs, df), BF)],
        got, w_tile, out, wd_f, hidden, name="delta_in",
    )
    got = exchange(message, "fsdp")
    message, dgu, dots = call(
        delta_body,
        [((n, fs + held, df), BF), ((2 * fs, slots), BF), ((l, h, LANES), F4)],
        got, gate, up, wgu, down, name="delta",
    )
    got = exchange(message, "fsdp")
    message, grad_down = call(
        back_body, [((l, 8 * h, df), BF), ((fs, d), F4)], got, dots, name="back"
    )
    got = exchange(message, "el")
    message, tick = call(
        combine_back_body,
        [((h, g + 8, df), BF), ((8, LANES), F4)],
        got, place, name="combine_back",
    )
    got = exchange(message, "eh")
    grad_gate, grad_up = call(
        grads_body, [((fs, d), F4)] * 2, tick, rows, dgu, name="grads"
    )
    grad_tokens, grad_route = call(
        finish_body, [((g, df), BF), ((8, g), F4)], got, expert_ids.T, name="finish"
    )
    return (
        layer_out, grad_tokens, grad_route.T, grad_gate[None], grad_up[None], grad_down[None]
    )


def solution(mesh):
    experts, fsdp = mesh.devices.shape
    split = Mesh(mesh.devices.reshape(HI, experts // HI, fsdp), ("eh", "el", "fsdp"))
    e = ("eh", "el")
    return jax.shard_map(
        shards,
        mesh=split,
        in_specs=(
            P(e, "fsdp"),
            P(e, "fsdp"),
            P(e, None),
            P(e, None),
            P(e, "fsdp", None),
            P(e, "fsdp", None),
            P(e, "fsdp", None),
        ),
        out_specs=(
            P(e, "fsdp"),
            P(e, "fsdp"),
            P(e, None),
            P(e, "fsdp", None),
            P(e, "fsdp", None),
            P(e, "fsdp", None),
        ),
        check_vma=False,
    )
```

```python
import functools

import jax
import jax.numpy as jnp
from jax import lax
from jax.experimental import pallas as pl
from jax.experimental.pallas import tpu as pltpu
from jax.sharding import Mesh, PartitionSpec as P

BF = jnp.bfloat16
F4 = jnp.float32
LANES = 128
HI = 8
CAP = 7


def dot(a, b, ca=1, cb=0):
    return lax.dot_general(a, b, (((ca,), (cb,)), ((), ())), preferred_element_type=F4)


def call(body, outs, *args, smem=(), hbm=(), scratch=(), vmem_mib=16, name=None):
    specs = [
        pl.BlockSpec(
            memory_space=pltpu.SMEM if i in smem else pltpu.HBM if i in hbm else pltpu.VMEM
        )
        for i in range(len(args))
    ]
    nbytes = sum(a.size * a.dtype.itemsize for a in args)
    shapes = [jax.ShapeDtypeStruct(s, d) for s, d in outs]
    return pl.pallas_call(
        body,
        out_shape=shapes,
        in_specs=specs,
        out_specs=[pl.BlockSpec(memory_space=pltpu.VMEM) for _ in shapes],
        scratch_shapes=list(scratch),
        compiler_params=pltpu.CompilerParams(vmem_limit_bytes=vmem_mib * 1024 * 1024),
        cost_estimate=pl.CostEstimate(
            flops=100_000_000, bytes_accessed=int(nbytes), transcendentals=0
        ),
        name=name,
    )(*args)


def lane(shape):
    return lax.broadcasted_iota(jnp.int32, shape, 1)


def roll(x, by):
    by = by % LANES
    return x if by == 0 else pltpu.roll(x, by, 1)


def split3(x, step):
    hi = x.astype(BF).astype(F4)
    rest = x - hi
    mid = rest.astype(BF).astype(F4)
    return hi + roll(mid, step) + roll(rest - mid, 2 * step)


def join3(x, step):
    return x + roll(x, -step) + roll(x, -2 * step)


def column_tile(column, h):
    at = lane((h, LANES))
    tile = jnp.zeros((h, LANES), F4)
    for c in range(CAP):
        tile = jnp.where(at == c, column[c * h : (c + 1) * h], tile)
    return tile


def scale_rows(rows, tile, h):
    return jnp.concatenate(
        [rows[c * h : (c + 1) * h] * tile[:, c : c + 1] for c in range(CAP)], axis=0
    )


def blocks_to_rows(x):
    return jnp.concatenate(
        [x[:, i * LANES : (i + 1) * LANES] for i in range(x.shape[1] // LANES)], axis=0
    )


def rows_to_blocks(x, rows):
    return jnp.concatenate(
        [x[i * rows : (i + 1) * rows] for i in range(x.shape[0] // rows)], axis=1
    )


def first_body(base_ref, ids_in, weights_in, t_in, m_ref, ids_ref, weights_ref, t_ref, sem):
    k, g = ids_ref.shape
    pairs = ((ids_in, ids_ref), (weights_in, weights_ref), (t_in, t_ref))
    copies = [pltpu.make_async_copy(a, b, sem.at[i]) for i, (a, b) in enumerate(pairs)]
    for copy in copies:
        copy.start()
    for copy in copies:
        copy.wait()
    w = weights_ref[...]
    hi = w.astype(BF)
    rest = w - hi.astype(F4)
    mid = rest.astype(BF)
    low = (rest - mid.astype(F4)).astype(BF)
    row = lax.broadcasted_iota(jnp.int32, (g, LANES), 0)
    col = lane((g, LANES))
    meta = jnp.zeros((k, LANES), F4)
    for i, part in enumerate((ids_ref[...].astype(F4).astype(BF), hi, mid, low)):
        move = jnp.where(col == row + i * g, 1.0, 0.0).astype(BF)
        meta = meta + dot(part, move)
    message = jnp.concatenate([t_ref[...].astype(F4), meta], axis=0).astype(BF)
    for i in range(m_ref.shape[0]):
        m_ref[i] = message


def weights_body(wg_ref, wu_ref, wd_ref, wgu_ref, wd_out_ref):
    fs = wg_ref.shape[0]
    wgu_ref[:fs] = wg_ref[...]
    wgu_ref[fs:] = wu_ref[...]
    wd_out_ref[...] = wd_ref[...]


def dispatch_body(base_ref, r_ref, m_ref, p_ref, ids_ref):
    h, l = r_ref.shape[0], m_ref.shape[0]
    g = 32
    width = h * g
    per = LANES // g
    at = lane((8, LANES))
    metas = [r_ref[i].astype(F4)[g : g + 8] for i in range(h)]

    def gathered(parts, start):
        out = []
        for q in range(h // per):
            acc = jnp.zeros((8, LANES), F4)
            for i in range(per):
                moved = roll(parts[q * per + i], i * g - start)
                acc = jnp.where(at // g == i, moved, acc)
            out.append(acc)
        return jnp.concatenate(out, axis=1)

    ids = gathered(metas, 0)
    weights = gathered([join3(m, g) for m in metas], g)
    ids_ref[...] = ids
    mine = (lax.broadcasted_iota(jnp.int32, (l, width), 0) + base_ref[0]).astype(F4)
    named = jnp.zeros((l, width), F4)
    weight_at = jnp.zeros((l, width), F4)
    for k in range(8):
        hit = ids[k : k + 1] == mine
        named = named + jnp.where(hit, 1.0, 0.0)
        weight_at = weight_at + jnp.where(hit, weights[k : k + 1], 0.0)
    row = lax.broadcasted_iota(jnp.int32, (width, width), 0)
    col = lane((width, width))
    before = jnp.where((row // g == col // g) & (row < col), 1.0, 0.0).astype(BF)
    rank = dot(named.astype(BF), before)
    rank = jnp.where(named > 0.0, rank, -1.0)
    block = lane((h, width)) // g == lax.broadcasted_iota(jnp.int32, (h, width), 0)
    x = jnp.concatenate([r_ref[i][:g] for i in range(h)], axis=0)
    for e in range(l):
        own = jnp.broadcast_to(rank[e : e + 1], (h, width))
        place = jnp.concatenate(
            [jnp.where(block & (own == float(c)), 1.0, 0.0) for c in range(8)], axis=0
        )
        column = jnp.sum(place * weight_at[e : e + 1], axis=1, keepdims=True)
        place = place.astype(BF)
        p_ref[e] = place
        rows = dot(place, x)
        tile = split3(column_tile(column, h), 8)
        m_ref[e] = jnp.concatenate([rows[: CAP * h], tile], axis=0).astype(BF)


def expert_in_body(r_ref, wd_ref, f_ref, w_ref):
    l, h = r_ref.shape[0], r_ref.shape[1] // 8
    fs = wd_ref.shape[0]
    rows = []
    for e in range(l):
        v = r_ref[e].astype(F4)
        rows.append(v[: CAP * h])
        w_ref[e] = join3(v[CAP * h :], 8)
    x = jnp.concatenate(rows, axis=0).astype(BF)
    for d in range(f_ref.shape[0]):
        f_ref[d, :fs] = wd_ref[:, d * LANES : (d + 1) * LANES]
        f_ref[d, fs:] = x


def hidden_body(r_ref, wgu_ref, gate_ref, up_ref, wd_ref, f_ref):
    n, fs = r_ref.shape[0], gate_ref.shape[0]
    slots = gate_ref.shape[1]
    held = r_ref.shape[1] - fs
    pad = jnp.zeros((slots - held, 2 * LANES), BF)
    total = jnp.zeros((2 * fs, slots), F4)
    for i in range(n // 2):
        x = jnp.concatenate([r_ref[2 * i, fs:], r_ref[2 * i + 1, fs:]], axis=1)
        x = jnp.concatenate([x, pad], axis=0)
        w = wgu_ref[:, 2 * i * LANES : 2 * (i + 1) * LANES]
        total = total + dot(w, x, 1, 1)
    gate, up = total[:fs], total[fs:]
    gate_ref[...] = gate
    up_ref[...] = up
    hidden = gate * jax.nn.sigmoid(gate) * up
    last = hidden[:, 3 * LANES :]
    last = last[: fs // 2] + roll(last[fs // 2 :], LANES // 2)
    message = blocks_to_rows(hidden[:, : 3 * LANES])
    message = jnp.concatenate([message, last], axis=0).astype(BF)
    for d in range(n):
        f_ref[d] = message
        wd_ref[d * fs : (d + 1) * fs] = r_ref[d, :fs]


def expert_out_body(r_ref, wd_ref, w_ref, out_ref, h_ref, m_ref):
    n, l, h = r_ref.shape[0], w_ref.shape[0], w_ref.shape[1]
    fs = wd_ref.shape[0] // n
    parts = []
    for i in range(n):
        v = r_ref[i].astype(F4)
        last = v[3 * fs :]
        left = lane(last.shape) < LANES // 2
        halves = [jnp.where(left, x, 0.0) for x in (last, roll(last, LANES // 2))]
        v = jnp.concatenate([v[: 3 * fs]] + halves, axis=0)
        parts.append(rows_to_blocks(v, fs).astype(BF))
    hidden = jnp.concatenate(parts, axis=0)
    h_ref[...] = hidden
    out = dot(hidden, wd_ref[...], 0, 0)
    out_ref[...] = out
    for e in range(l):
        rows = out[e * CAP * h : (e + 1) * CAP * h]
        rows = scale_rows(rows, w_ref[e], h)
        m_ref[e] = jnp.concatenate([rows, jnp.zeros((h, LANES), F4)], axis=0).astype(BF)


def combine_body(r_ref, p_ref, m_ref):
    l, rows = r_ref.shape[0], r_ref.shape[1]
    x = jnp.concatenate([r_ref[i] for i in range(l)], axis=0)
    p = jnp.concatenate([p_ref[i] for i in range(l)], axis=0)
    y = dot(p, x, 0, 0).astype(BF)
    g = m_ref.shape[1]
    for i in range(m_ref.shape[0]):
        m_ref[i] = y[i * g : (i + 1) * g]


def resid_body(r_ref, t_ref, o_ref, m_ref):
    total = r_ref[0].astype(F4)
    for i in range(1, r_ref.shape[0]):
        total = total + r_ref[i].astype(F4)
    layer = total.astype(BF)
    o_ref[...] = layer
    resid = (layer.astype(F4) - t_ref[...].astype(F4)).astype(BF)
    for i in range(m_ref.shape[0]):
        m_ref[i] = resid


def redispatch_body(r_ref, p_ref, m_ref):
    x = jnp.concatenate([r_ref[i] for i in range(r_ref.shape[0])], axis=0)
    for e in range(p_ref.shape[0]):
        m_ref[e] = dot(p_ref[e], x)[: m_ref.shape[1]].astype(BF)


def delta_in_body(r_ref, w_ref, out_ref, wd_ref, h_ref, f_ref, g_ref):
    l, h = w_ref.shape[0], w_ref.shape[1]
    n, fs = f_ref.shape[0], f_ref.shape[1] // 4
    slots = h_ref.shape[1]
    rows, tiles = [], []
    for e in range(l):
        resid = r_ref[e].astype(F4)[: CAP * h]
        out = out_ref[e * CAP * h : (e + 1) * CAP * h]
        column = jnp.sum(resid * out, axis=1, keepdims=True)
        tiles.append(split3(column_tile(column, h), 8))
        rows.append(scale_rows(resid, w_ref[e], h))
    rows.append(jnp.zeros((slots - l * CAP * h, LANES), F4))
    scaled = jnp.concatenate(rows, axis=0).astype(BF)
    half = l // 2
    packed = roll(jnp.concatenate(tiles[:half], axis=0), 64) + roll(
        jnp.concatenate(tiles[half:], axis=0), 88
    )
    packed = jnp.concatenate([packed, jnp.zeros((fs - packed.shape[0], LANES), F4)], axis=0)
    parts = dot(wd_ref[...], scaled, 1, 1)
    down = dot(h_ref[...], scaled)
    for d in range(n):
        part = parts[d * fs : (d + 1) * fs]
        message = blocks_to_rows(part)
        last = message[3 * fs :] + packed
        f_ref[d] = jnp.concatenate([message[: 3 * fs], last], axis=0).astype(BF)
        g_ref[d] = down[d * fs : (d + 1) * fs].astype(BF)


def delta_body(r_ref, gate_ref, up_ref, wgu_ref, gd_ref, f_ref, dgu_ref, dot_ref):
    n, fs = f_ref.shape[0], gate_ref.shape[0]
    l, h = dot_ref.shape[0], dot_ref.shape[1]
    total = r_ref[0].astype(F4)
    for i in range(1, n):
        total = total + r_ref[i].astype(F4)
    packed = total[3 * fs : 3 * fs + l * h // 2]
    first, second = join3(roll(packed, -64), 8), join3(roll(packed, -88), 8)
    at = lane((h, LANES))
    for e in range(l):
        source = first if e < l // 2 else second
        i = e % (l // 2)
        dot_ref[e] = jnp.where(at < CAP, source[i * h : (i + 1) * h], 0.0)
    dh = rows_to_blocks(total, fs)
    gate, up = gate_ref[...], up_ref[...]
    s = jax.nn.sigmoid(gate)
    dgate = (dh * up * s * (1.0 + gate * (1.0 - s))).astype(BF)
    dup = (dh * gate * s).astype(BF)
    dgu = jnp.concatenate([dgate, dup], axis=0)
    dgu_ref[...] = dgu
    held = CAP * h * l
    for i in range(n // 2):
        back = dot(dgu, wgu_ref[:, 2 * i * LANES : 2 * (i + 1) * LANES], 0, 0)
        back = back[:held].astype(BF)
        for d in (2 * i, 2 * i + 1):
            own = (d - 2 * i) * LANES
            f_ref[d, :fs] = gd_ref[d]
            f_ref[d, fs:] = back[:, own : own + LANES]


def back_body(r_ref, dot_ref, m_ref, gd_ref):
    l, h = dot_ref.shape[0], dot_ref.shape[1]
    fs = r_ref.shape[1] - CAP * h * l
    total = r_ref[0, fs:].astype(F4)
    for i in range(1, r_ref.shape[0]):
        total = total + r_ref[i, fs:].astype(F4)
    for e in range(l):
        rows = total[e * CAP * h : (e + 1) * CAP * h]
        m_ref[e] = jnp.concatenate([rows, split3(dot_ref[e], 8)], axis=0).astype(BF)
    for i in range(r_ref.shape[0]):
        gd_ref[:, i * LANES : (i + 1) * LANES] = r_ref[i, :fs].astype(F4)


def grads_body(tick_ref, x_ref, dgu_ref, gg_ref, gu_ref):
    n, fs = x_ref.shape[0], gg_ref.shape[0]
    dgu = dgu_ref[...]
    pad = jnp.zeros((dgu.shape[1] - x_ref.shape[1] + fs, 2 * LANES), BF)
    for i in range(n // 2):
        x = jnp.concatenate([x_ref[2 * i, fs:], x_ref[2 * i + 1, fs:]], axis=1)
        grad = dot(dgu, jnp.concatenate([x, pad], axis=0))
        part = pl.ds(2 * i * LANES, 2 * LANES)
        gg_ref[:, part] = grad[:fs]
        gu_ref[:, part] = grad[fs:]


def combine_back_body(base_ref, r_ref, p_ref, ids_ref, m_ref, tick_ref):
    l, hosts = r_ref.shape[0], m_ref.shape[0]
    h = hosts
    g = 32
    per = LANES // g
    x = jnp.concatenate([r_ref[i] for i in range(l)], axis=0)
    p = jnp.concatenate([p_ref[i] for i in range(l)], axis=0)
    y = dot(p, x, 0, 0)
    ids = ids_ref[...]
    tick_ref[...] = ids[:, :LANES]
    routes = jnp.zeros(ids.shape, F4)
    for e in range(l):
        tile = join3(r_ref[e].astype(F4)[CAP * h :], 8)
        place = p_ref[e].astype(F4)
        acc = jnp.zeros((h, ids.shape[1]), F4)
        for c in range(CAP):
            acc = acc + place[c * h : (c + 1) * h] * tile[:, c : c + 1]
        at_token = jnp.sum(acc, axis=0, keepdims=True)
        mine = (base_ref[0] + e).astype(F4)
        routes = routes + jnp.where(ids == mine, at_token, 0.0)
    at = lane((8, LANES))
    for i in range(hosts):
        q = i // per
        own = roll(routes[:, q * LANES : (q + 1) * LANES], -(i % per) * g)
        own = split3(jnp.where(at < g, own, 0.0), g)
        m_ref[i] = jnp.concatenate([y[i * g : (i + 1) * g], own], axis=0).astype(BF)


def finish_body(r_ref, t_ref, g_ref):
    total = r_ref[0].astype(F4)
    for i in range(1, r_ref.shape[0]):
        total = total + r_ref[i].astype(F4)
    rows = t_ref.shape[0]
    t_ref[...] = total[:rows].astype(BF)
    g_ref[...] = join3(total[rows : rows + 8], rows)[:, :rows]


def exchange(x, axis):
    return lax.all_to_all(x, axis, split_axis=0, concat_axis=0, tiled=True)


def shards(tokens, target, expert_ids, route_weights, w_gate, w_up, w_down):
    h, l, n = lax.axis_size("eh"), lax.axis_size("el"), lax.axis_size("fsdp")
    g, k = expert_ids.shape
    fs, d = w_gate.shape[1], w_gate.shape[2]
    df = tokens.shape[1]
    mean_load = k * g // (h * l)
    assert df == LANES and g == 32 and k == 8 and h % 8 == 0
    assert min(g, mean_load + mean_load // 2 + 1) == CAP
    wg, wu, wd = w_gate[0], w_up[0], w_down[0]
    held, slots = CAP * h * l, 8 * h * l
    base = (lax.axis_index("eh") * l).astype(jnp.int32).reshape(1)

    (message,) = call(
        first_body, [((h, g + 8, df), BF)],
        base, expert_ids.T, route_weights.T, tokens, smem=(0,), hbm=(1, 2, 3),
        scratch=(
            pltpu.VMEM((k, g), jnp.int32), pltpu.VMEM((k, g), F4), pltpu.VMEM((g, df), BF),
            pltpu.SemaphoreType.DMA((3,)),
        ),
        vmem_mib=60, name="first",
    )
    got = exchange(message, "eh")
    wgu, wd = call(
        weights_body, [((2 * fs, d), BF), ((fs, d), BF)], wg, wu, wd, name="weights"
    )
    message, place, ids = call(
        dispatch_body,
        [((l, 8 * h, df), BF), ((l, 8 * h, h * g), BF), ((8, h * g), F4)],
        base, got, smem=(0,), name="dispatch",
    )
    got = exchange(message, "el")
    message, w_tile = call(
        expert_in_body,
        [((n, fs + held, df), BF), ((l, h, LANES), F4)],
        got, wd, name="expert_in",
    )
    rows = exchange(message, "fsdp")
    packed = (n, fs * slots // LANES, LANES)
    half_packed = (n, fs * slots // LANES - fs // 2, LANES)
    gate, up, wd_f, message = call(
        hidden_body,
        [((fs, slots), F4), ((fs, slots), F4), ((n * fs, df), BF), (half_packed, BF)],
        rows, wgu, name="hidden",
    )
    got = exchange(message, "fsdp")
    out, hidden, message = call(
        expert_out_body,
        [((slots, df), F4), ((n * fs, slots), BF), ((l, 8 * h, df), BF)],
        got, wd_f, w_tile, name="expert_out",
    )
    got = exchange(message, "el")
    (message,) = call(combine_body, [((h, g, df), BF)], got, place, name="combine")
    got = exchange(message, "eh")
    layer_out, message = call(
        resid_body, [((g, df), BF), ((h, g, df), BF)], got, target, name="resid"
    )
    got = exchange(message, "eh")
    (message,) = call(
        redispatch_body, [((l, CAP * h, df), BF)], got, place, name="redispatch"
    )
    got = exchange(message, "el")
    message, down = call(
        delta_in_body,
        [(packed, BF), ((n, fs, df), BF)],
        got, w_tile, out, wd_f, hidden, name="delta_in",
    )
    got = exchange(message, "fsdp")
    message, dgu, dots = call(
        delta_body,
        [((n, fs + held, df), BF), ((2 * fs, slots), BF), ((l, h, LANES), F4)],
        got, gate, up, wgu, down, name="delta",
    )
    got = exchange(message, "fsdp")
    message, grad_down = call(
        back_body, [((l, 8 * h, df), BF), ((fs, d), F4)], got, dots, name="back"
    )
    got = exchange(message, "el")
    message, tick = call(
        combine_back_body,
        [((h, g + 8, df), BF), ((8, LANES), F4)],
        base, got, place, ids, smem=(0,), name="combine_back",
    )
    got = exchange(message, "eh")
    grad_gate, grad_up = call(
        grads_body, [((fs, d), F4)] * 2, tick, rows, dgu, name="grads"
    )
    grad_tokens, grad_route = call(
        finish_body, [((g, df), BF), ((8, g), F4)], got, name="finish"
    )
    return (
        layer_out, grad_tokens, grad_route.T, grad_gate[None], grad_up[None], grad_down[None]
    )


def solution(mesh):
    experts, fsdp = mesh.devices.shape
    split = Mesh(mesh.devices.reshape(HI, experts // HI, fsdp), ("eh", "el", "fsdp"))
    e = ("eh", "el")
    return jax.shard_map(
        shards,
        mesh=split,
        in_specs=(
            P(e, "fsdp"),
            P(e, "fsdp"),
            P(e, None),
            P(e, None),
            P(e, "fsdp", None),
            P(e, "fsdp", None),
            P(e, "fsdp", None),
        ),
        out_specs=(
            P(e, "fsdp"),
            P(e, "fsdp"),
            P(e, None),
            P(e, "fsdp", None),
            P(e, "fsdp", None),
            P(e, "fsdp", None),
        ),
        check_vma=False,
    )
```

```python
import functools

import jax
import jax.numpy as jnp
from jax import lax
from jax.experimental import pallas as pl
from jax.experimental.pallas import tpu as pltpu
from jax.sharding import Mesh, PartitionSpec as P

BF = jnp.bfloat16
F4 = jnp.float32
LANES = 128
HI = 8
CAP = 7


def dot(a, b, ca=1, cb=0):
    return lax.dot_general(a, b, (((ca,), (cb,)), ((), ())), preferred_element_type=F4)


def call(body, outs, *args, smem=(), hbm=(), scratch=(), vmem_mib=16, name=None):
    specs = [
        pl.BlockSpec(
            memory_space=pltpu.SMEM if i in smem else pltpu.HBM if i in hbm else pltpu.VMEM
        )
        for i in range(len(args))
    ]
    nbytes = sum(a.size * a.dtype.itemsize for a in args)
    shapes = [jax.ShapeDtypeStruct(s, d) for s, d in outs]
    return pl.pallas_call(
        body,
        out_shape=shapes,
        in_specs=specs,
        out_specs=[pl.BlockSpec(memory_space=pltpu.VMEM) for _ in shapes],
        scratch_shapes=list(scratch),
        compiler_params=pltpu.CompilerParams(vmem_limit_bytes=vmem_mib * 1024 * 1024),
        cost_estimate=pl.CostEstimate(
            flops=100_000_000, bytes_accessed=int(nbytes), transcendentals=0
        ),
        name=name,
    )(*args)


def lane(shape):
    return lax.broadcasted_iota(jnp.int32, shape, 1)


def roll(x, by):
    by = by % LANES
    return x if by == 0 else pltpu.roll(x, by, 1)


def split3(x, step):
    hi = x.astype(BF).astype(F4)
    rest = x - hi
    mid = rest.astype(BF).astype(F4)
    return hi + roll(mid, step) + roll(rest - mid, 2 * step)


def join3(x, step):
    return x + roll(x, -step) + roll(x, -2 * step)


def column_tile(column, h):
    at = lane((h, LANES))
    tile = jnp.zeros((h, LANES), F4)
    for c in range(CAP):
        tile = jnp.where(at == c, column[c * h : (c + 1) * h], tile)
    return tile


def scale_rows(rows, tile, h):
    return jnp.concatenate(
        [rows[c * h : (c + 1) * h] * tile[:, c : c + 1] for c in range(CAP)], axis=0
    )


def blocks_to_rows(x):
    return jnp.concatenate(
        [x[:, i * LANES : (i + 1) * LANES] for i in range(x.shape[1] // LANES)], axis=0
    )


def rows_to_blocks(x, rows):
    return jnp.concatenate(
        [x[i * rows : (i + 1) * rows] for i in range(x.shape[0] // rows)], axis=1
    )


def first_body(base_ref, ids_in, weights_in, t_in, m_ref, ids_ref, weights_ref, t_ref, sem):
    k, g = ids_ref.shape
    pairs = ((ids_in, ids_ref), (weights_in, weights_ref), (t_in, t_ref))
    copies = [pltpu.make_async_copy(a, b, sem.at[i]) for i, (a, b) in enumerate(pairs)]
    for copy in copies:
        copy.start()
    for copy in copies:
        copy.wait()
    w = weights_ref[...]
    hi = w.astype(BF)
    rest = w - hi.astype(F4)
    mid = rest.astype(BF)
    low = (rest - mid.astype(F4)).astype(BF)
    row = lax.broadcasted_iota(jnp.int32, (g, LANES), 0)
    col = lane((g, LANES))
    meta = jnp.zeros((k, LANES), F4)
    for i, part in enumerate((ids_ref[...].astype(F4).astype(BF), hi, mid, low)):
        move = jnp.where(col == row + i * g, 1.0, 0.0).astype(BF)
        meta = meta + dot(part, move)
    message = jnp.concatenate([t_ref[...].astype(F4), meta], axis=0).astype(BF)
    for i in range(m_ref.shape[0]):
        m_ref[i] = message


def weights_body(wg_ref, wu_ref, wd_ref, wgu_ref, wd_out_ref, tick_ref):
    fs = wg_ref.shape[0]
    wgu_ref[:fs] = wg_ref[...]
    wgu_ref[fs:] = wu_ref[...]
    wd_out_ref[...] = wd_ref[...]
    tick_ref[...] = jnp.zeros_like(tick_ref)


def dispatch_body(base_ref, r_ref, tick_ref, m_ref, p_ref, ids_ref):
    h, l = r_ref.shape[0], m_ref.shape[0]
    g = 32
    width = h * g
    per = LANES // g
    at = lane((8, LANES))
    metas = [r_ref[i].astype(F4)[g : g + 8] for i in range(h)]

    def gathered(parts, start):
        out = []
        for q in range(h // per):
            acc = jnp.zeros((8, LANES), F4)
            for i in range(per):
                moved = roll(parts[q * per + i], i * g - start)
                acc = jnp.where(at // g == i, moved, acc)
            out.append(acc)
        return jnp.concatenate(out, axis=1)

    ids = gathered(metas, 0)
    weights = gathered([join3(m, g) for m in metas], g)
    ids_ref[...] = ids
    mine = (lax.broadcasted_iota(jnp.int32, (l, width), 0) + base_ref[0]).astype(F4)
    named = jnp.zeros((l, width), F4)
    weight_at = jnp.zeros((l, width), F4)
    for k in range(8):
        hit = ids[k : k + 1] == mine
        named = named + jnp.where(hit, 1.0, 0.0)
        weight_at = weight_at + jnp.where(hit, weights[k : k + 1], 0.0)
    row = lax.broadcasted_iota(jnp.int32, (width, width), 0)
    col = lane((width, width))
    before = jnp.where((row // g == col // g) & (row < col), 1.0, 0.0).astype(BF)
    rank = dot(named.astype(BF), before)
    rank = jnp.where(named > 0.0, rank, -1.0)
    block = lane((h, width)) // g == lax.broadcasted_iota(jnp.int32, (h, width), 0)
    x = jnp.concatenate([r_ref[i][:g] for i in range(h)], axis=0)
    for e in range(l):
        own = jnp.broadcast_to(rank[e : e + 1], (h, width))
        place = jnp.concatenate(
            [jnp.where(block & (own == float(c)), 1.0, 0.0) for c in range(8)], axis=0
        )
        column = jnp.sum(place * weight_at[e : e + 1], axis=1, keepdims=True)
        place = place.astype(BF)
        p_ref[e] = place
        rows = dot(place, x)
        tile = split3(column_tile(column, h), 8)
        m_ref[e] = jnp.concatenate([rows[: CAP * h], tile], axis=0).astype(BF)


def expert_in_body(r_ref, wd_ref, f_ref, w_ref):
    l, h = r_ref.shape[0], r_ref.shape[1] // 8
    fs = wd_ref.shape[0]
    rows = []
    for e in range(l):
        v = r_ref[e].astype(F4)
        rows.append(v[: CAP * h])
        w_ref[e] = join3(v[CAP * h :], 8)
    x = jnp.concatenate(rows, axis=0).astype(BF)
    for d in range(f_ref.shape[0]):
        f_ref[d, :fs] = wd_ref[:, d * LANES : (d + 1) * LANES]
        f_ref[d, fs:] = x


def hidden_body(r_ref, wgu_ref, gate_ref, up_ref, wd_ref, f_ref):
    n, fs = r_ref.shape[0], gate_ref.shape[0]
    slots = gate_ref.shape[1]
    held = r_ref.shape[1] - fs
    pad = jnp.zeros((slots - held, 2 * LANES), BF)
    total = jnp.zeros((2 * fs, slots), F4)
    for i in range(n // 2):
        x = jnp.concatenate([r_ref[2 * i, fs:], r_ref[2 * i + 1, fs:]], axis=1)
        x = jnp.concatenate([x, pad], axis=0)
        w = wgu_ref[:, 2 * i * LANES : 2 * (i + 1) * LANES]
        total = total + dot(w, x, 1, 1)
    gate, up = total[:fs], total[fs:]
    gate_ref[...] = gate
    up_ref[...] = up
    hidden = gate * jax.nn.sigmoid(gate) * up
    last = hidden[:, 3 * LANES :]
    last = last[: fs // 2] + roll(last[fs // 2 :], LANES // 2)
    message = blocks_to_rows(hidden[:, : 3 * LANES])
    message = jnp.concatenate([message, last], axis=0).astype(BF)
    for d in range(n):
        f_ref[d] = message
        wd_ref[d * fs : (d + 1) * fs] = r_ref[d, :fs]


def expert_out_body(r_ref, wd_ref, w_ref, out_ref, h_ref, m_ref):
    n, l, h = r_ref.shape[0], w_ref.shape[0], w_ref.shape[1]
    fs = wd_ref.shape[0] // n
    parts = []
    for i in range(n):
        v = r_ref[i].astype(F4)
        last = v[3 * fs :]
        left = lane(last.shape) < LANES // 2
        halves = [jnp.where(left, x, 0.0) for x in (last, roll(last, LANES // 2))]
        v = jnp.concatenate([v[: 3 * fs]] + halves, axis=0)
        parts.append(rows_to_blocks(v, fs).astype(BF))
    hidden = jnp.concatenate(parts, axis=0)
    h_ref[...] = hidden
    out = dot(hidden, wd_ref[...], 0, 0)
    out_ref[...] = out
    for e in range(l):
        rows = out[e * CAP * h : (e + 1) * CAP * h]
        rows = scale_rows(rows, w_ref[e], h)
        m_ref[e] = jnp.concatenate([rows, jnp.zeros((h, LANES), F4)], axis=0).astype(BF)


def combine_body(r_ref, p_ref, m_ref):
    l, rows = r_ref.shape[0], r_ref.shape[1]
    x = jnp.concatenate([r_ref[i] for i in range(l)], axis=0)
    p = jnp.concatenate([p_ref[i] for i in range(l)], axis=0)
    y = dot(p, x, 0, 0).astype(BF)
    g = m_ref.shape[1]
    for i in range(m_ref.shape[0]):
        m_ref[i] = y[i * g : (i + 1) * g]


def resid_body(r_ref, t_ref, o_ref, m_ref):
    total = r_ref[0].astype(F4)
    for i in range(1, r_ref.shape[0]):
        total = total + r_ref[i].astype(F4)
    layer = total.astype(BF)
    o_ref[...] = layer
    resid = (layer.astype(F4) - t_ref[...].astype(F4)).astype(BF)
    for i in range(m_ref.shape[0]):
        m_ref[i] = resid


def redispatch_body(r_ref, p_ref, m_ref):
    x = jnp.concatenate([r_ref[i] for i in range(r_ref.shape[0])], axis=0)
    for e in range(p_ref.shape[0]):
        m_ref[e] = dot(p_ref[e], x)[: m_ref.shape[1]].astype(BF)


def delta_in_body(r_ref, w_ref, out_ref, wd_ref, h_ref, f_ref, g_ref):
    l, h = w_ref.shape[0], w_ref.shape[1]
    n, fs = f_ref.shape[0], f_ref.shape[1] // 4
    slots = h_ref.shape[1]
    rows, tiles = [], []
    for e in range(l):
        resid = r_ref[e].astype(F4)[: CAP * h]
        out = out_ref[e * CAP * h : (e + 1) * CAP * h]
        column = jnp.sum(resid * out, axis=1, keepdims=True)
        tiles.append(split3(column_tile(column, h), 8))
        rows.append(scale_rows(resid, w_ref[e], h))
    rows.append(jnp.zeros((slots - l * CAP * h, LANES), F4))
    scaled = jnp.concatenate(rows, axis=0).astype(BF)
    half = l // 2
    packed = roll(jnp.concatenate(tiles[:half], axis=0), 64) + roll(
        jnp.concatenate(tiles[half:], axis=0), 88
    )
    packed = jnp.concatenate([packed, jnp.zeros((fs - packed.shape[0], LANES), F4)], axis=0)
    parts = dot(wd_ref[...], scaled, 1, 1)
    down = dot(h_ref[...], scaled)
    for d in range(n):
        part = parts[d * fs : (d + 1) * fs]
        message = blocks_to_rows(part)
        last = message[3 * fs :] + packed
        f_ref[d] = jnp.concatenate([message[: 3 * fs], last], axis=0).astype(BF)
        g_ref[d] = down[d * fs : (d + 1) * fs].astype(BF)


def delta_body(r_ref, gate_ref, up_ref, wgu_ref, gd_ref, f_ref, dgu_ref, dot_ref):
    n, fs = f_ref.shape[0], gate_ref.shape[0]
    l, h = dot_ref.shape[0], dot_ref.shape[1]
    total = r_ref[0].astype(F4)
    for i in range(1, n):
        total = total + r_ref[i].astype(F4)
    packed = total[3 * fs : 3 * fs + l * h // 2]
    first, second = join3(roll(packed, -64), 8), join3(roll(packed, -88), 8)
    at = lane((h, LANES))
    for e in range(l):
        source = first if e < l // 2 else second
        i = e % (l // 2)
        dot_ref[e] = jnp.where(at < CAP, source[i * h : (i + 1) * h], 0.0)
    dh = rows_to_blocks(total, fs)
    gate, up = gate_ref[...], up_ref[...]
    s = jax.nn.sigmoid(gate)
    dgate = (dh * up * s * (1.0 + gate * (1.0 - s))).astype(BF)
    dup = (dh * gate * s).astype(BF)
    dgu = jnp.concatenate([dgate, dup], axis=0)
    dgu_ref[...] = dgu
    held = CAP * h * l
    for i in range(n // 2):
        back = dot(dgu, wgu_ref[:, 2 * i * LANES : 2 * (i + 1) * LANES], 0, 0)
        back = back[:held].astype(BF)
        for d in (2 * i, 2 * i + 1):
            own = (d - 2 * i) * LANES
            f_ref[d, :fs] = gd_ref[d]
            f_ref[d, fs:] = back[:, own : own + LANES]


def back_body(r_ref, dot_ref, m_ref, gd_ref):
    l, h = dot_ref.shape[0], dot_ref.shape[1]
    fs = r_ref.shape[1] - CAP * h * l
    total = r_ref[0, fs:].astype(F4)
    for i in range(1, r_ref.shape[0]):
        total = total + r_ref[i, fs:].astype(F4)
    for e in range(l):
        rows = total[e * CAP * h : (e + 1) * CAP * h]
        m_ref[e] = jnp.concatenate([rows, split3(dot_ref[e], 8)], axis=0).astype(BF)
    for i in range(r_ref.shape[0]):
        gd_ref[:, i * LANES : (i + 1) * LANES] = r_ref[i, :fs].astype(F4)


def grads_body(tick_ref, x_ref, dgu_ref, gg_ref, gu_ref):
    n, fs = x_ref.shape[0], gg_ref.shape[0]
    dgu = dgu_ref[...]
    pad = jnp.zeros((dgu.shape[1] - x_ref.shape[1] + fs, 2 * LANES), BF)
    for i in range(n // 2):
        x = jnp.concatenate([x_ref[2 * i, fs:], x_ref[2 * i + 1, fs:]], axis=1)
        grad = dot(dgu, jnp.concatenate([x, pad], axis=0))
        part = pl.ds(2 * i * LANES, 2 * LANES)
        gg_ref[:, part] = grad[:fs]
        gu_ref[:, part] = grad[fs:]


def combine_back_body(base_ref, r_ref, p_ref, ids_ref, m_ref, tick_ref):
    l, hosts = r_ref.shape[0], m_ref.shape[0]
    h = hosts
    g = 32
    per = LANES // g
    x = jnp.concatenate([r_ref[i] for i in range(l)], axis=0)
    p = jnp.concatenate([p_ref[i] for i in range(l)], axis=0)
    y = dot(p, x, 0, 0)
    ids = ids_ref[...]
    tick_ref[...] = ids[:, :LANES]
    routes = jnp.zeros(ids.shape, F4)
    for e in range(l):
        tile = join3(r_ref[e].astype(F4)[CAP * h :], 8)
        place = p_ref[e].astype(F4)
        acc = jnp.zeros((h, ids.shape[1]), F4)
        for c in range(CAP):
            acc = acc + place[c * h : (c + 1) * h] * tile[:, c : c + 1]
        at_token = jnp.sum(acc, axis=0, keepdims=True)
        mine = (base_ref[0] + e).astype(F4)
        routes = routes + jnp.where(ids == mine, at_token, 0.0)
    at = lane((8, LANES))
    for i in range(hosts):
        q = i // per
        own = roll(routes[:, q * LANES : (q + 1) * LANES], -(i % per) * g)
        own = split3(jnp.where(at < g, own, 0.0), g)
        m_ref[i] = jnp.concatenate([y[i * g : (i + 1) * g], own], axis=0).astype(BF)


def finish_body(r_ref, t_ref, g_ref):
    total = r_ref[0].astype(F4)
    for i in range(1, r_ref.shape[0]):
        total = total + r_ref[i].astype(F4)
    rows = t_ref.shape[0]
    t_ref[...] = total[:rows].astype(BF)
    g_ref[...] = join3(total[rows : rows + 8], rows)[:, :rows]


def exchange(x, axis):
    return lax.all_to_all(x, axis, split_axis=0, concat_axis=0, tiled=True)


def shards(tokens, target, expert_ids, route_weights, w_gate, w_up, w_down):
    h, l, n = lax.axis_size("eh"), lax.axis_size("el"), lax.axis_size("fsdp")
    g, k = expert_ids.shape
    fs, d = w_gate.shape[1], w_gate.shape[2]
    df = tokens.shape[1]
    mean_load = k * g // (h * l)
    assert df == LANES and g == 32 and k == 8 and h % 8 == 0
    assert min(g, mean_load + mean_load // 2 + 1) == CAP
    wg, wu, wd = w_gate[0], w_up[0], w_down[0]
    held, slots = CAP * h * l, 8 * h * l
    base = (lax.axis_index("eh") * l).astype(jnp.int32).reshape(1)

    (message,) = call(
        first_body, [((h, g + 8, df), BF)],
        base, expert_ids.T, route_weights.T, tokens, smem=(0,), hbm=(1, 2, 3),
        scratch=(
            pltpu.VMEM((k, g), jnp.int32), pltpu.VMEM((k, g), F4), pltpu.VMEM((g, df), BF),
            pltpu.SemaphoreType.DMA((3,)),
        ),
        vmem_mib=60, name="first",
    )
    got = exchange(message, "eh")
    wgu, wd, tick = call(
        weights_body, [((2 * fs, d), BF), ((fs, d), BF), ((8, LANES), F4)], wg, wu, wd, name="weights"
    )
    message, place, ids = call(
        dispatch_body,
        [((l, 8 * h, df), BF), ((l, 8 * h, h * g), BF), ((8, h * g), F4)],
        base, got, tick, smem=(0,), name="dispatch",
    )
    got = exchange(message, "el")
    message, w_tile = call(
        expert_in_body,
        [((n, fs + held, df), BF), ((l, h, LANES), F4)],
        got, wd, name="expert_in",
    )
    rows = exchange(message, "fsdp")
    packed = (n, fs * slots // LANES, LANES)
    half_packed = (n, fs * slots // LANES - fs // 2, LANES)
    gate, up, wd_f, message = call(
        hidden_body,
        [((fs, slots), F4), ((fs, slots), F4), ((n * fs, df), BF), (half_packed, BF)],
        rows, wgu, name="hidden",
    )
    got = exchange(message, "fsdp")
    out, hidden, message = call(
        expert_out_body,
        [((slots, df), F4), ((n * fs, slots), BF), ((l, 8 * h, df), BF)],
        got, wd_f, w_tile, name="expert_out",
    )
    got = exchange(message, "el")
    (message,) = call(combine_body, [((h, g, df), BF)], got, place, name="combine")
    got = exchange(message, "eh")
    layer_out, message = call(
        resid_body, [((g, df), BF), ((h, g, df), BF)], got, target, name="resid"
    )
    got = exchange(message, "eh")
    (message,) = call(
        redispatch_body, [((l, CAP * h, df), BF)], got, place, name="redispatch"
    )
    got = exchange(message, "el")
    message, down = call(
        delta_in_body,
        [(packed, BF), ((n, fs, df), BF)],
        got, w_tile, out, wd_f, hidden, name="delta_in",
    )
    got = exchange(message, "fsdp")
    message, dgu, dots = call(
        delta_body,
        [((n, fs + held, df), BF), ((2 * fs, slots), BF), ((l, h, LANES), F4)],
        got, gate, up, wgu, down, name="delta",
    )
    got = exchange(message, "fsdp")
    message, grad_down = call(
        back_body, [((l, 8 * h, df), BF), ((fs, d), F4)], got, dots, name="back"
    )
    got = exchange(message, "el")
    message, tick = call(
        combine_back_body,
        [((h, g + 8, df), BF), ((8, LANES), F4)],
        base, got, place, ids, smem=(0,), name="combine_back",
    )
    got = exchange(message, "eh")
    grad_gate, grad_up = call(
        grads_body, [((fs, d), F4)] * 2, tick, rows, dgu, name="grads"
    )
    grad_tokens, grad_route = call(
        finish_body, [((g, df), BF), ((8, g), F4)], got, name="finish"
    )
    return (
        layer_out, grad_tokens, grad_route.T, grad_gate[None], grad_up[None], grad_down[None]
    )


def solution(mesh):
    experts, fsdp = mesh.devices.shape
    split = Mesh(mesh.devices.reshape(HI, experts // HI, fsdp), ("eh", "el", "fsdp"))
    e = ("eh", "el")
    return jax.shard_map(
        shards,
        mesh=split,
        in_specs=(
            P(e, "fsdp"),
            P(e, "fsdp"),
            P(e, None),
            P(e, None),
            P(e, "fsdp", None),
            P(e, "fsdp", None),
            P(e, "fsdp", None),
        ),
        out_specs=(
            P(e, "fsdp"),
            P(e, "fsdp"),
            P(e, None),
            P(e, "fsdp", None),
            P(e, "fsdp", None),
            P(e, "fsdp", None),
        ),
        check_vma=False,
    )
```
